256 devices in a mesh: context: 16 (over y, z_hi, core), tensor: 16 (over z_lo, x).
Axes of the slice: x: 4, y: 4, z: 8 (z_hi: 2, z_lo: 4; z = z_hi * 4 + z_lo), core: 2. Of those that a mesh axis runs over, the one named last changes fastest.
Arguments:
- queries: bfloat16 [2048, 6144], P('context', 'tensor')
- context_keys: bfloat16 [4096, 1024], P('context')
- context_values: bfloat16 [4096, 1024], P('context'), may hold values from -6 to 6
- query_span: int32 [2048], replicated, may hold values from 0 to 31
- query_position: int32 [2048], replicated, may hold values from 0 to 16383
- key_span: int32 [4096], replicated, may hold values from 0 to 31
- key_position: int32 [4096], replicated, may hold values from 0 to 16383
- tile_table: int32 [16, 32], replicated, may hold values 0 or 1
- residual: bfloat16 [2048, 7168], P('tensor', 'context')
- out_weight: bfloat16 [6144, 7168], P('tensor', 'context'), may hold values from -0.078125 to 0.078125
- norm_gain: bfloat16 [7168], P('context'), may hold values from 0.099609375 to 1.8984375
- gate_weight: bfloat16 [7168, 19200], P('context', 'tensor'), may hold values from -0.0625 to 0.0625
- up_weight: bfloat16 [7168, 19200], P('context', 'tensor'), may hold values from -0.0625 to 0.0625
- down_weight: bfloat16 [19200, 7168], P('tensor', 'context'), may hold values from -0.046875 to 0.046875
Outputs:
- attention: bfloat16 [2048, 6144], P('context', 'tensor')
- mixed: bfloat16 [2048, 7168], P('tensor', 'context')
The draws below stay inside these ranges and needn't reach their ends.
All inputs are finite; a program needn't handle non-finite values.
Results may differ from the reference program's by a relative error of at most 0.022.
Values may be sent and summed in bfloat16 or wider, within the bound.
A program may use at most 128 MiB of HBM per device.

```python
import math
import jax
import jax.numpy as jnp
from jax import lax

D = 7168
FF = 19200
HEADS = 48
KVH = 8
DH = 128
TILE = 128
SINK = 4
SPANS = 32
POS_RANGE = 16384
QTOK = 2048
CTX = 4096
N_CONTEXT = 16
N_TENSOR = 16


def draw_context_keys(key, part):
    key = jax.random.fold_in(key, 11)
    entries = jax.random.normal(key, (CTX, KVH * DH), jnp.float32)
    return entries.astype(jnp.bfloat16)


def draw_queries(key, part):
    key = jax.random.fold_in(key, 12)
    entry_key = jax.random.fold_in(key, 0)
    entries = jax.random.normal(entry_key, (QTOK, HEADS * DH), jnp.float32) * 1.5
    return entries.astype(jnp.bfloat16)


def draw_residual(key, part):
    key = jax.random.fold_in(key, 13)
    row_key, entry_key = jax.random.split(key)
    column_scale = 0.4 * jnp.power(10.0, jnp.arange(D, dtype=jnp.float32) / D)
    row_scale = jnp.exp(jax.random.uniform(row_key, (QTOK, 1), jnp.float32, math.log(0.5), math.log(2.0)))
    entries = jax.random.normal(entry_key, (QTOK, D), jnp.float32)
    return (entries * row_scale * column_scale[None, :]).astype(jnp.bfloat16)


def place_ends(drawn, own_key, low, high):
    longest = drawn.shape.index(max(drawn.shape))
    spots = []
    for shift in (0, 1):
        where = [jax.random.randint(jax.random.fold_in(own_key, axis), (), 0, length) for axis, length in enumerate(drawn.shape)]
        where[longest] = (where[longest] + shift) % drawn.shape[longest]
        spots.append(tuple(where))
    return drawn.at[spots[0]].set(low).at[spots[1]].set(high)


def levels(rng, dims, cuts, low, high):
    gain = 1.0
    for dim, shards_of in cuts:
        draws = jax.random.uniform(jax.random.fold_in(jax.random.fold_in(rng, 6), dim), (shards_of,), jnp.float32, low / len(cuts), high / len(cuts))
        gain = gain * jnp.repeat(jnp.exp(draws), dims[dim] // shards_of).reshape((-1,) + (1,) * (len(dims) - 1 - dim))
    return gain


def scatter_about(stream_key, extent, scale, reach, cuts=(), kind=jnp.bfloat16):
    loudness = levels(stream_key, extent, cuts, -0.22, 0.18) if cuts else 1.0
    result = jax.random.normal(stream_key, extent, jnp.float32) * scale * loudness
    return jnp.minimum(jnp.maximum(result, -reach), reach).astype(kind)


def setup_inputs(seed: int = 0) -> dict:
    streams_of = jax.random.split(jax.random.key(seed), 15)
    return {
        "queries": draw_queries(jax.random.fold_in(streams_of[14], 71), 0),
        "context_keys": draw_context_keys(jax.random.fold_in(streams_of[14], 71), 0),
        "context_values": scatter_about(streams_of[2], (CTX, KVH * DH), 1.0, 6.0, ((0, 16),)),
        "query_span": place_ends(jax.random.randint(streams_of[3], (QTOK,), 0, SPANS), jax.random.fold_in(streams_of[3], 1), 0, SPANS - 1).astype(jnp.int32),
        "query_position": place_ends(jax.random.randint(streams_of[4], (QTOK,), 0, POS_RANGE), jax.random.fold_in(streams_of[4], 1), 0, POS_RANGE - 1).astype(jnp.int32),
        "key_span": place_ends(jax.random.randint(streams_of[5], (CTX,), 0, SPANS), jax.random.fold_in(streams_of[5], 1), 0, SPANS - 1).astype(jnp.int32),
        "key_position": place_ends(jax.random.randint(streams_of[6], (CTX,), 0, POS_RANGE), jax.random.fold_in(streams_of[6], 1), 0, POS_RANGE - 1).astype(jnp.int32),
        "tile_table": place_ends((jax.random.randint(streams_of[7], (QTOK // TILE, CTX // TILE), 0, 2) < 1).astype(jnp.int32), jax.random.fold_in(streams_of[7], 1), 0, 1),
        "residual": draw_residual(jax.random.fold_in(streams_of[14], 71), 0),
        "out_weight": scatter_about(streams_of[9], (HEADS * DH, D), (HEADS * DH) ** -0.5, 0.078125, ((0, 16), (1, 16))),
        "norm_gain": jnp.clip(1.0 + 0.18 * jax.random.normal(streams_of[10], (D,), jnp.float32), 0.099609375, 1.8984375).astype(jnp.bfloat16),
        "gate_weight": scatter_about(streams_of[11], (D, FF), D ** -0.5, 0.0625, ((0, 16), (1, 16))),
        "up_weight": scatter_about(streams_of[12], (D, FF), D ** -0.5, 0.0625, ((0, 16), (1, 16))),
        "down_weight": scatter_about(streams_of[13], (FF, D), FF ** -0.5, 0.046875, ((0, 16), (1, 16))),
    }


blocked_score = -1e+30

def reference(queries, context_keys, context_values, query_span, query_position, key_span, key_position, tile_table, residual, out_weight, norm_gain, gate_weight, up_weight, down_weight):
    grouped = HEADS // KVH
    key_total = context_keys.shape[0]
    row_total = queries.shape[0]
    keys_all = context_keys.astype(jnp.float32).reshape(key_total, KVH, DH)
    values_all = context_values.astype(jnp.float32).reshape(key_total, KVH, DH)
    key_index = jnp.arange(key_total, dtype=jnp.int32)
    key_tile = key_index // TILE

    def one_tile(tile_number):
        first_row = (tile_number * TILE).astype(jnp.int32)
        query_block = lax.dynamic_slice_in_dim(queries, first_row, TILE, 0).astype(jnp.float32).reshape(TILE, KVH, grouped, DH)
        row_spans = lax.dynamic_slice_in_dim(query_span, first_row, TILE, 0)
        places = lax.dynamic_slice_in_dim(query_position, first_row, TILE, 0)
        allowed = tile_table[tile_number][key_tile]
        visible = (key_index[None, :] < SINK) | (allowed[None, :] == 1) & (key_span[None, :] == row_spans[:, None]) & (key_position[None, :] < places[:, None])
        visible_wide = visible[:, None, None, :]
        scores = jnp.einsum('qgad,kgd->qgak', query_block, keys_all) / math.sqrt(DH)
        scores = jnp.where(visible_wide, scores, blocked_score)
        highest = lax.optimization_barrier(jnp.max(scores, axis=-1, keepdims=True))
        weights = jnp.where(visible_wide, jnp.exp(scores - highest), 0.0)
        totals = lax.optimization_barrier(jnp.sum(weights, axis=-1))
        rounded = lax.optimization_barrier(weights.astype(jnp.bfloat16)).astype(jnp.float32)
        attended = jnp.einsum('qgak,kgd->qgad', rounded, values_all) / totals[..., None]
        return attended.reshape(TILE, HEADS * DH).astype(jnp.bfloat16)
    attention = lax.map(one_tile, jnp.arange(row_total // TILE, dtype=jnp.int32)).reshape(row_total, HEADS * DH)
    head_width = HEADS // N_TENSOR * DH
    projected = jnp.zeros((row_total, D), jnp.float32)
    for group_number in range(N_TENSOR):
        lower = group_number * head_width
        partial_term = jnp.dot(attention[:, lower:lower + head_width], out_weight[lower:lower + head_width], preferred_element_type=jnp.float32)
        projected = projected + lax.optimization_barrier(partial_term.astype(jnp.bfloat16)).astype(jnp.float32)
    summed = (residual.astype(jnp.float32) + projected).astype(jnp.bfloat16)
    stream = summed.astype(jnp.float32)
    mean_square = lax.optimization_barrier(jnp.mean(stream * stream, axis=1, keepdims=True))
    normed = (stream * lax.rsqrt(mean_square + 1e-05) * norm_gain.astype(jnp.float32)).astype(jnp.bfloat16)
    column_slab = D // N_CONTEXT
    gate_sum = jnp.zeros((row_total, FF), jnp.float32)
    up_sum = jnp.zeros((row_total, FF), jnp.float32)
    for group_number in range(N_CONTEXT):
        lower = group_number * column_slab
        gate_part = jnp.dot(normed[:, lower:lower + column_slab], gate_weight[lower:lower + column_slab], preferred_element_type=jnp.float32)
        up_part = jnp.dot(normed[:, lower:lower + column_slab], up_weight[lower:lower + column_slab], preferred_element_type=jnp.float32)
        gate_sum = gate_sum + lax.optimization_barrier(gate_part.astype(jnp.bfloat16)).astype(jnp.float32)
        up_sum = up_sum + lax.optimization_barrier(up_part.astype(jnp.bfloat16)).astype(jnp.float32)
    hidden = (jax.nn.silu(gate_sum) * up_sum).astype(jnp.bfloat16)
    hidden_slab = FF // N_TENSOR
    down_sum = jnp.zeros((row_total, D), jnp.float32)
    for group_number in range(N_TENSOR):
        lower = group_number * hidden_slab
        down_part = jnp.dot(hidden[:, lower:lower + hidden_slab], down_weight[lower:lower + hidden_slab], preferred_element_type=jnp.float32)
        down_sum = down_sum + lax.optimization_barrier(down_part.astype(jnp.bfloat16)).astype(jnp.float32)
    mixed = (stream + down_sum).astype(jnp.bfloat16)
    return (attention, mixed)
```

```python
import math

import jax
import jax.numpy as jnp
from jax import lax
from jax.experimental import pallas as pl
from jax.experimental.pallas import tpu as pltpu
from jax.sharding import PartitionSpec as P

MESH = pl.DeviceIdType.MESH
F32 = jnp.float32
BF16 = jnp.bfloat16

D = 7168
DH = 128
TILE = 128
SINK = 4
ROWS = 128
HALF = ROWS // 2
NH = 3
KROWS = 256
COLS = 448
CC = 2 * COLS
FF = 1200
BLOCKS = 8

BLOCKED = -1e30
SCORE_SCALE = math.log2(math.e) / math.sqrt(DH)

N_COPIES = 140


def layer_kernel(
    q_ref,
    key_ref,
    value_ref,
    qspan_ref,
    qpos_ref,
    kspan_ref,
    kpos_ref,
    table_ref,
    res_ref,
    wo_ref,
    gain_ref,
    wg_ref,
    wu_ref,
    wd_ref,
    att_out,
    mix_out,
    kv,
    q3,
    m_s,
    l_s,
    acc_s,
    att,
    wo_in,
    wo2,
    wd_in,
    wd2,
    wg2,
    wu2,
    res2,
    gain2,
    part,
    half_in,
    full_in,
    z_out,
    z_in,
    stream,
    sq_out,
    sq_in,
    normed,
    gu,
    gu_half,
    gu_full,
    gu_z,
    hid,
    part2,
    half_in2,
    full_in2,
    z_out2,
    z_in2,
    mix_send,
    mix_recv,
    send_sem,
    recv_sem,
    local_sem,
):
    c = lax.axis_index("context")
    t = lax.axis_index("tensor")
    y, z, k = c // 4, lax.rem(c // 2, 2), lax.rem(c, 2)
    zl, x = t // 4, lax.rem(t, 4)
    yp, ym, yo = lax.rem(y + 1, 4), lax.rem(y + 3, 4), lax.rem(y + 2, 4)
    xp, xm = lax.rem(x + 1, 4), lax.rem(x + 3, 4)
    zo, ko = 1 - z, 1 - k

    def dev(y_=None, z_=None, k_=None, zl_=None, x_=None):
        y_ = y if y_ is None else y_
        z_ = z if z_ is None else z_
        k_ = k if k_ is None else k_
        zl_ = zl if zl_ is None else zl_
        x_ = x if x_ is None else x_
        return (4 * y_ + 2 * z_ + k_, 4 * zl_ + x_)

    sibling, across = dev(k_=ko), dev(z_=zo)
    up_y, down_y = dev(y_=yp), dev(y_=ym)
    up_x, down_x = dev(x_=xp), dev(x_=xm)
    zl_peers = [dev(zl_=lax.rem(zl + d, 4)) for d in (1, 2, 3)]
    norm_peers = [
        dev(y_=lax.rem(y + dy, 4), z_=lax.rem(z + dz, 2))
        for dy in range(4)
        for dz in range(2)
        if dy or dz
    ]
    is_home = lax.rem(x + k, 2) == 0
    is_relay = lax.rem(x + k, 2) == 1

    count = [0]
    sent = []

    def new_id():
        count[0] += 1
        return count[0] - 1

    def copy(src, dst, to, number):
        return pltpu.make_async_remote_copy(
            src_ref=src,
            dst_ref=dst,
            send_sem=send_sem.at[number],
            recv_sem=recv_sem.at[number],
            device_id=to,
            device_id_type=MESH,
        )

    def send(src, dst, to, number):
        one = copy(src, dst, to, number)
        one.start()
        sent.append(one)

    def arrived(dst, number):
        copy(dst, dst, sibling, number).wait_recv()

    kv_head = t // 2
    head_columns = pl.ds(pl.multiple_of(kv_head * DH, DH), DH)
    loads = [
        pltpu.make_async_copy(key_ref.at[:, head_columns], kv.at[c, :, 0:DH], local_sem.at[0]),
        pltpu.make_async_copy(
            value_ref.at[:, head_columns], kv.at[c, :, DH : 2 * DH], local_sem.at[1]
        ),
        pltpu.make_async_copy(wo_ref, wo_in.at[k], local_sem.at[2]),
        pltpu.make_async_copy(res_ref, res2.at[k], local_sem.at[3]),
        pltpu.make_async_copy(gain_ref, gain2.at[k], local_sem.at[4]),
        pltpu.make_async_copy(
            wg_ref, wg2.at[pl.ds(pl.multiple_of(k * COLS, COLS), COLS)], local_sem.at[5]
        ),
        pltpu.make_async_copy(
            wu_ref, wu2.at[pl.ds(pl.multiple_of(k * COLS, COLS), COLS)], local_sem.at[6]
        ),
        pltpu.make_async_copy(wd_ref, wd_in.at[k], local_sem.at[7]),
    ]
    for one in loads:
        one.start()

    barrier = pltpu.get_barrier_semaphore()
    peers = [sibling, up_x, down_x] + zl_peers + norm_peers
    for peer in peers:
        pl.semaphore_signal(barrier, inc=1, device_id=peer, device_id_type=MESH)
    pl.semaphore_wait(barrier, len(peers))

    loads[0].wait()
    loads[1].wait()
    ids = [new_id() for _ in range(17)]

    def block_at(y_, z_, k_):
        return kv.at[4 * y_ + 2 * z_ + k_]

    def half_at(y_, z_, k_, h):
        return kv.at[4 * y_ + 2 * z_ + k_, h * (KROWS // 2) : (h + 1) * (KROWS // 2)]

    own = block_at(y, z, k)
    send(own, own, across, ids[0])
    send(own, own, up_y, ids[1])
    send(own, own, down_y, ids[2])
    send(own, own, sibling, ids[3])

    for one in loads[2:]:
        one.wait()
    weight_ids = [new_id() for _ in range(6)]
    half_rows = pl.ds(pl.multiple_of(k * COLS, COLS), COLS)
    other_rows = pl.ds(pl.multiple_of(ko * COLS, COLS), COLS)

    other = block_at(y, zo, k)
    arrived(other, ids[0])
    send(other, other, up_y, ids[4])
    send(other, other, down_y, ids[5])
    send(other, other, sibling, ids[6])
    b = block_at(ym, z, k)
    arrived(b, ids[1])
    send(half_at(ym, z, k, 0), half_at(ym, z, k, 0), up_y, ids[7])
    send(b, b, sibling, ids[9])
    b = block_at(yp, z, k)
    arrived(b, ids[2])
    send(half_at(yp, z, k, 1), half_at(yp, z, k, 1), down_y, ids[8])
    send(b, b, sibling, ids[10])
    b = block_at(ym, zo, k)
    arrived(b, ids[4])
    send(half_at(ym, zo, k, 0), half_at(ym, zo, k, 0), up_y, ids[11])
    send(b, b, sibling, ids[13])
    b = block_at(yp, zo, k)
    arrived(b, ids[5])
    send(half_at(yp, zo, k, 1), half_at(yp, zo, k, 1), down_y, ids[12])
    send(b, b, sibling, ids[14])

    for h in range(NH):
        q3[h] = q_ref[:, h * DH : (h + 1) * DH]
    m_s[...] = jnp.full(m_s.shape, BLOCKED, F32)
    l_s[...] = jnp.zeros(l_s.shape, F32)
    acc_s[...] = jnp.zeros(acc_s.shape, F32)

    def as_column(row):
        return jnp.broadcast_to(row.astype(F32), (ROWS, ROWS)).T.astype(jnp.int32)

    q_span = as_column(qspan_ref[pl.ds(c, 1), :])
    q_pos = as_column(qpos_ref[pl.ds(c, 1), :])

    def attend(group):
        visible = []
        for n in range(8):
            tile = 8 * group + n
            allowed = table_ref[c, tile] == 1
            spans = jnp.where(allowed, kspan_ref[pl.ds(tile, 1), :], -1)
            places = kpos_ref[pl.ds(tile, 1), :]
            index = tile * TILE + lax.broadcasted_iota(jnp.int32, (1, TILE), 1)
            spans = jnp.broadcast_to(spans, (ROWS, TILE))
            places = jnp.broadcast_to(places, (ROWS, TILE))
            index = jnp.broadcast_to(index, (ROWS, TILE))
            visible.append(
                jnp.where(
                    ((spans == q_span) & (places < q_pos)) | (index < SINK), 0.0, BLOCKED
                ).astype(F32)
            )
        keys = kv[pl.ds(4 * group, 4)].reshape(4 * KROWS, 2 * DH)

        def one_head(h, carry):
            scores = lax.dot_general(
                q3[h], keys[:, :DH], (((1,), (1,)), ((), ())), preferred_element_type=F32
            )
            pieces = [
                jnp.where(
                    visible[n] == 0.0,
                    scores[:, n * TILE : (n + 1) * TILE] * SCORE_SCALE,
                    BLOCKED,
                )
                for n in range(8)
            ]
            best = pieces[0]
            for piece in pieces[1:]:
                best = jnp.maximum(best, piece)
            old = m_s[h]
            new = jnp.maximum(old, jnp.max(best, axis=1, keepdims=True))
            factor = jnp.exp2(old - new)
            weights = [jnp.exp2(piece - new) for piece in pieces]
            total = weights[0]
            for one in weights[1:]:
                total = total + one
            m_s[h] = new
            l_s[h] = l_s[h] * factor + total
            rounded = jnp.concatenate([one.astype(BF16) for one in weights], axis=1)
            acc_s[h] = acc_s[h] * factor + jnp.dot(
                rounded, keys[:, DH:], preferred_element_type=F32
            )
            return carry

        lax.fori_loop(0, NH, one_head, 0)

    arrived(block_at(y, z, ko), ids[3])
    arrived(block_at(y, zo, ko), ids[6])
    attend(y)

    arrived(half_at(yo, z, k, 0), ids[7])
    arrived(half_at(yo, z, k, 1), ids[8])
    b = block_at(yo, z, k)
    send(b, b, sibling, ids[15])
    arrived(half_at(yo, zo, k, 0), ids[11])
    arrived(half_at(yo, zo, k, 1), ids[12])
    b = block_at(yo, zo, k)
    send(b, b, sibling, ids[16])

    arrived(block_at(ym, z, ko), ids[9])
    arrived(block_at(ym, zo, ko), ids[13])
    attend(ym)
    arrived(block_at(yp, z, ko), ids[10])
    arrived(block_at(yp, zo, ko), ids[14])
    attend(yp)
    arrived(block_at(yo, z, ko), ids[15])
    arrived(block_at(yo, zo, ko), ids[16])
    attend(yo)

    mine = 2 * y + z
    for h in range(NH):
        total = jnp.sum(l_s[h], axis=1, keepdims=True)
        att[mine, :, h * DH : (h + 1) * DH] = (acc_s[h] / total).astype(BF16)

    def gather_context(buf, ready):
        ids = [new_id() for _ in range(9)]

        def whole(y_, z_):
            return buf.at[2 * y_ + z_]

        def part_of(y_, z_, h):
            return buf.at[2 * y_ + z_, h * HALF : (h + 1) * HALF]

        own = whole(y, z)
        send(own, own, across, ids[0])
        send(own, own, up_y, ids[1])
        send(own, own, down_y, ids[2])
        ready(2 * y + z)
        b = whole(y, zo)
        arrived(b, ids[0])
        send(b, b, up_y, ids[3])
        send(b, b, down_y, ids[4])
        arrived(whole(ym, z), ids[1])
        send(part_of(ym, z, 0), part_of(ym, z, 0), up_y, ids[5])
        arrived(whole(yp, z), ids[2])
        send(part_of(yp, z, 1), part_of(yp, z, 1), down_y, ids[6])
        ready(2 * y + zo)
        ready(2 * ym + z)
        ready(2 * yp + z)
        arrived(whole(ym, zo), ids[3])
        send(part_of(ym, zo, 0), part_of(ym, zo, 0), up_y, ids[7])
        arrived(whole(yp, zo), ids[4])
        send(part_of(yp, zo, 1), part_of(yp, zo, 1), down_y, ids[8])
        ready(2 * ym + zo)
        ready(2 * yp + zo)
        arrived(part_of(yo, z, 0), ids[5])
        arrived(part_of(yo, z, 1), ids[6])
        ready(2 * yo + z)
        arrived(part_of(yo, zo, 0), ids[7])
        arrived(part_of(yo, zo, 1), ids[8])
        ready(2 * yo + zo)

    send(wo_in.at[k], wo_in.at[k], sibling, weight_ids[0])
    send(res2.at[k], res2.at[k], sibling, weight_ids[1])
    send(gain2.at[k], gain2.at[k], sibling, weight_ids[2])
    send(wg2.at[half_rows], wg2.at[half_rows], sibling, weight_ids[3])
    send(wu2.at[half_rows], wu2.at[half_rows], sibling, weight_ids[4])
    send(wd_in.at[k], wd_in.at[k], sibling, weight_ids[5])

    first = [True]

    def project(i):
        if first[0]:
            first[0] = False
            arrived(wo_in.at[ko], weight_ids[0])
            wo2[...] = jnp.concatenate([wo_in[0], wo_in[1]], axis=1)
        part[i] = jnp.dot(att[i], wo2[...], preferred_element_type=F32).astype(BF16)

    gather_context(att, project)
    att_out[...] = att[mine]

    home_j = x // 2
    plus_j, minus_j = xp // 2, xm // 2

    def scatter_tensor(shares, halves, fulls, out, inn, finish):
        half_ids = [[new_id() for _ in range(2)] for _ in range(4)]
        full_ids = [[new_id() for _ in range(2)] for _ in range(4)]
        z_ids = [new_id() for _ in range(3)]
        order = [(d, lax.rem(zl + d, 4)) for d in (2, 1, 3, 0)]

        @pl.when(is_home)
        def _():
            kept = list(sent)
            sent.clear()
            for d, to in order:
                i = 2 * to + 1 - home_j
                send(shares.at[i, 0:HALF], halves.at[0, to], up_x, half_ids[d][0])
                send(shares.at[i, HALF:ROWS], halves.at[1, to], down_x, half_ids[d][1])
            total = None
            for d, to in order:
                arrived(fulls.at[0, to], full_ids[d][0])
                arrived(fulls.at[1, to], full_ids[d][1])
                here = (
                    shares[2 * to + home_j].astype(F32)
                    + fulls[0, to].astype(F32)
                    + fulls[1, to].astype(F32)
                )
                if d:
                    out[d - 1] = here.astype(BF16)
                    send(out.at[d - 1], inn.at[d - 1], zl_peers[d - 1], z_ids[d - 1])
                else:
                    total = here
            for d in (1, 3, 2):
                arrived(inn.at[d - 1], z_ids[d - 1])
                total = total + inn[d - 1].astype(F32)
            finish(total)
            for one in sent:
                one.wait_send()
            sent.clear()
            sent.extend(kept)

        @pl.when(is_relay)
        def _():
            kept = list(sent)
            sent.clear()
            for d, to in order:
                i = 2 * to + plus_j
                arrived(halves.at[0, to], half_ids[d][0])
                shares[i, 0:HALF] = (
                    shares[i, 0:HALF].astype(F32) + halves[0, to].astype(F32)
                ).astype(BF16)
                send(shares.at[i], fulls.at[0, to], up_x, full_ids[d][0])
                i = 2 * to + minus_j
                arrived(halves.at[1, to], half_ids[d][1])
                shares[i, HALF:ROWS] = (
                    shares[i, HALF:ROWS].astype(F32) + halves[1, to].astype(F32)
                ).astype(BF16)
                send(shares.at[i], fulls.at[1, to], down_x, full_ids[d][1])
            for one in sent:
                one.wait_send()
            sent.clear()
            sent.extend(kept)

    arrived(res2.at[ko], weight_ids[1])
    arrived(gain2.at[ko], weight_ids[2])
    norm_ids = [new_id() for _ in range(7)]
    gather_z = [new_id() for _ in range(3)]
    gather_x = [[new_id() for _ in range(2)] for _ in range(4)]
    gather_half = [[new_id() for _ in range(2)] for _ in range(4)]

    def normalise(total):
        res = jnp.concatenate([res2[0].astype(F32), res2[1].astype(F32)], axis=1)
        rounded = (res + total).astype(BF16)
        stream[...] = rounded
        st = rounded.astype(F32)
        squares = jnp.sum(st * st, axis=1, keepdims=True)
        sq_out[...] = jnp.broadcast_to(squares, (ROWS, ROWS)).T[0:8]
        for n, peer in enumerate(norm_peers):
            send(sq_out, sq_in.at[n], peer, norm_ids[n])
        whole = sq_out[...]
        for n in range(7):
            arrived(sq_in.at[n], norm_ids[n])
            whole = whole + sq_in[n]
        column = jnp.broadcast_to(whole[0:1], (ROWS, ROWS)).T[:, 0:1]
        gain = jnp.concatenate([gain2[0][0:1], gain2[1][0:1]], axis=1)
        i = 2 * zl + home_j
        normed[i] = (st * lax.rsqrt(column / D + 1e-05) * gain).astype(BF16)
        own = normed.at[i]
        for d in (1, 2, 3):
            send(own, own, zl_peers[d - 1], gather_z[d - 1])
        for d in (0, 1, 3, 2):
            b = normed.at[2 * lax.rem(zl + 4 - d, 4) + home_j]
            if d:
                arrived(b, gather_z[d - 1])
            send(b, b, up_x, gather_x[d][0])
            send(b, b, down_x, gather_x[d][1])
        for d in (0, 1, 3, 2):
            i = 2 * lax.rem(zl + 4 - d, 4) + 1 - home_j
            arrived(normed.at[i, 0:HALF], gather_half[d][0])
            arrived(normed.at[i, HALF:ROWS], gather_half[d][1])

    scatter_tensor(part, half_in, full_in, z_out, z_in, normalise)

    @pl.when(is_relay)
    def _():
        kept = list(sent)
        sent.clear()
        for d in (0, 1, 3, 2):
            i = 2 * lax.rem(zl + 4 - d, 4) + minus_j
            arrived(normed.at[i], gather_x[d][0])
            send(normed.at[i, 0:HALF], normed.at[i, 0:HALF], up_x, gather_half[d][0])
            i = 2 * lax.rem(zl + 4 - d, 4) + plus_j
            arrived(normed.at[i], gather_x[d][1])
            send(normed.at[i, HALF:ROWS], normed.at[i, HALF:ROWS], down_x, gather_half[d][1])
        for one in sent:
            one.wait_send()
        sent.clear()
        sent.extend(kept)

    arrived(wg2.at[other_rows], weight_ids[3])
    arrived(wu2.at[other_rows], weight_ids[4])

    def gate_up(i):
        rows = normed[i]
        gu[i, 0] = jnp.dot(rows, wg2[...], preferred_element_type=F32).astype(BF16)
        gu[i, 1] = jnp.dot(rows, wu2[...], preferred_element_type=F32).astype(BF16)

    first_ids = [[new_id() for _ in range(2)] for _ in range(2)]
    second_ids = [[new_id() for _ in range(2)] for _ in range(2)]
    cross_id = new_id()
    z_order = [(0, zo), (1, z)]

    def far(n, carry):
        gate_up(2 * yo + lax.rem(z + 1 + n, 2))
        return carry

    def near(n, carry):
        gate_up(2 * lax.rem(y + 1 + 2 * lax.rem(n, 2), 4) + lax.rem(z + 1 + n // 2, 2))
        return carry

    def own_rows(n, carry):
        gate_up(2 * y + lax.rem(z + 1 + n, 2))
        return carry

    lax.fori_loop(0, 2, far, 0)
    for n, zz in z_order:
        i = 2 * yo + zz
        send(gu.at[i, :, 0:HALF], gu_half.at[0, n], up_y, first_ids[n][0])
        send(gu.at[i, :, HALF:ROWS], gu_half.at[1, n], down_y, first_ids[n][1])
    lax.fori_loop(0, 4, near, 0)
    for n, zz in z_order:
        i = 2 * yp + zz
        arrived(gu_half.at[0, n], first_ids[n][0])
        gu[i, :, 0:HALF] = (gu[i, :, 0:HALF].astype(F32) + gu_half[0, n].astype(F32)).astype(BF16)
        send(gu.at[i], gu_full.at[0, n], up_y, second_ids[n][0])
        i = 2 * ym + zz
        arrived(gu_half.at[1, n], first_ids[n][1])
        gu[i, :, HALF:ROWS] = (
            gu[i, :, HALF:ROWS].astype(F32) + gu_half[1, n].astype(F32)
        ).astype(BF16)
        send(gu.at[i], gu_full.at[1, n], down_y, second_ids[n][1])
    lax.fori_loop(0, 2, own_rows, 0)
    arrived(wd_in.at[ko], weight_ids[5])
    wd2[...] = jnp.concatenate([wd_in[0], wd_in[1]], axis=1)

    def own_sum(n, zz, which):
        return (
            gu[2 * y + zz, which].astype(F32)
            + gu_full[0, n, which].astype(F32)
            + gu_full[1, n, which].astype(F32)
        )

    arrived(gu_full.at[0, 0], second_ids[0][0])
    arrived(gu_full.at[1, 0], second_ids[0][1])
    gu[2 * y + zo, 0] = own_sum(0, zo, 0).astype(BF16)
    gu[2 * y + zo, 1] = own_sum(0, zo, 1).astype(BF16)
    send(gu.at[2 * y + zo], gu_z, across, cross_id)
    arrived(gu_full.at[0, 1], second_ids[1][0])
    arrived(gu_full.at[1, 1], second_ids[1][1])
    arrived(gu_z, cross_id)
    gate = own_sum(1, z, 0) + gu_z[0].astype(F32)
    up = own_sum(1, z, 1) + gu_z[1].astype(F32)
    hid[mine] = (gate / (1.0 + jnp.exp(-gate)) * up).astype(BF16)

    def down(i):
        part2[i] = jnp.dot(hid[i], wd2[...], preferred_element_type=F32).astype(BF16)

    gather_context(hid, down)

    mix_id = new_id()

    def mix(total):
        mixed = stream[...].astype(F32) + total
        low, high = mixed[:, :COLS], mixed[:, COLS:]
        mix_out[...] = jnp.where(k == 0, low, high).astype(BF16)
        mix_send[...] = jnp.where(k == 0, high, low).astype(BF16)
        send(mix_send, mix_recv, sibling, mix_id)

    scatter_tensor(part2, half_in2, full_in2, z_out2, z_in2, mix)

    @pl.when(is_relay)
    def _():
        arrived(mix_recv, mix_id)
        mix_out[...] = mix_recv[...]

    for one in sent:
        one.wait_send()
    assert count[0] <= N_COPIES


def local(
    queries,
    context_keys,
    context_values,
    query_span,
    query_position,
    key_span,
    key_position,
    tile_table,
    residual,
    out_weight,
    norm_gain,
    gate_weight,
    up_weight,
    down_weight,
):
    vmem = pl.BlockSpec(memory_space=pltpu.VMEM)
    smem = pl.BlockSpec(memory_space=pltpu.SMEM)
    hbm = pl.BlockSpec(memory_space=pl.ANY)
    gain = jnp.broadcast_to(norm_gain.astype(F32)[None, :], (8, COLS))
    scratch = [
        pltpu.VMEM((16, KROWS, 2 * DH), BF16),
        pltpu.VMEM((NH, ROWS, DH), BF16),
        pltpu.VMEM((NH, ROWS, DH), F32),
        pltpu.VMEM((NH, ROWS, DH), F32),
        pltpu.VMEM((NH, ROWS, DH), F32),
        pltpu.VMEM((BLOCKS, ROWS, NH * DH), BF16),
        pltpu.VMEM((2, NH * DH, COLS), BF16),
        pltpu.VMEM((NH * DH, CC), BF16),
        pltpu.VMEM((2, FF, COLS), BF16),
        pltpu.VMEM((FF, CC), BF16),
        pltpu.VMEM((CC, FF), BF16),
        pltpu.VMEM((CC, FF), BF16),
        pltpu.VMEM((2, ROWS, COLS), BF16),
        pltpu.VMEM((2, 8, COLS), F32),
        pltpu.VMEM((BLOCKS, ROWS, CC), BF16),
        pltpu.VMEM((2, 4, HALF, CC), BF16),
        pltpu.VMEM((2, 4, ROWS, CC), BF16),
        pltpu.VMEM((3, ROWS, CC), BF16),
        pltpu.VMEM((3, ROWS, CC), BF16),
        pltpu.VMEM((ROWS, CC), BF16),
        pltpu.VMEM((8, ROWS), F32),
        pltpu.VMEM((7, 8, ROWS), F32),
        pltpu.VMEM((BLOCKS, ROWS, CC), BF16),
        pltpu.VMEM((BLOCKS, 2, ROWS, FF), BF16),
        pltpu.VMEM((2, 2, 2, HALF, FF), BF16),
        pltpu.VMEM((2, 2, 2, ROWS, FF), BF16),
        pltpu.VMEM((2, ROWS, FF), BF16),
        pltpu.VMEM((BLOCKS, ROWS, FF), BF16),
        pltpu.VMEM((BLOCKS, ROWS, CC), BF16),
        pltpu.VMEM((2, 4, HALF, CC), BF16),
        pltpu.VMEM((2, 4, ROWS, CC), BF16),
        pltpu.VMEM((3, ROWS, CC), BF16),
        pltpu.VMEM((3, ROWS, CC), BF16),
        pltpu.VMEM((ROWS, COLS), BF16),
        pltpu.VMEM((ROWS, COLS), BF16),
        pltpu.SemaphoreType.DMA((N_COPIES,)),
        pltpu.SemaphoreType.DMA((N_COPIES,)),
        pltpu.SemaphoreType.DMA((8,)),
    ]
    return pl.pallas_call(
        layer_kernel,
        out_shape=(
            jax.ShapeDtypeStruct(queries.shape, BF16),
            jax.ShapeDtypeStruct(residual.shape, BF16),
        ),
        in_specs=[vmem, hbm, hbm, vmem, vmem, vmem, vmem, smem, hbm, hbm, hbm, hbm, hbm, hbm],
        out_specs=(vmem, vmem),
        scratch_shapes=scratch,
        compiler_params=pltpu.CompilerParams(
            collective_id=0, has_side_effects=True, vmem_limit_bytes=60 * 2**20
        ),
        cost_estimate=pl.CostEstimate(
            flops=9_000_000_000, bytes_accessed=8_000_000, transcendentals=2_000_000
        ),
        name="layer",
    )(
        queries,
        context_keys,
        context_values,
        query_span.reshape(16, TILE),
        query_position.reshape(16, TILE),
        key_span.reshape(32, TILE),
        key_position.reshape(32, TILE),
        tile_table,
        residual,
        out_weight,
        gain,
        gate_weight,
        up_weight,
        down_weight,
    )


def solution(mesh):
    placed = (
        P("context", "tensor"),
        P("context", None),
        P("context", None),
        P(),
        P(),
        P(),
        P(),
        P(),
        P("tensor", "context"),
        P("tensor", "context"),
        P("context"),
        P("context", "tensor"),
        P("context", "tensor"),
        P("tensor", "context"),
    )
    return jax.shard_map(
        local,
        mesh=mesh,
        in_specs=placed,
        out_specs=(P("context", "tensor"), P("tensor", "context")),
        check_vma=False,
    )
```

```python
import math

import jax
import jax.numpy as jnp
from jax import lax
from jax.experimental import pallas as pl
from jax.experimental.pallas import tpu as pltpu
from jax.sharding import PartitionSpec as P

MESH = pl.DeviceIdType.MESH
F32 = jnp.float32
BF16 = jnp.bfloat16

D = 7168
DH = 128
TILE = 128
SINK = 4
ROWS = 128
HALF = ROWS // 2
QUARTER = HALF // 2
NH = 3
KROWS = 256
COLS = 448
CC = 2 * COLS
FF = 1200
BLOCKS = 8

BLOCKED = -1e30
SCORE_SCALE = math.log2(math.e) / math.sqrt(DH)

N_COPIES = 260


def layer_kernel(
    q_ref,
    key_ref,
    value_ref,
    qspan_ref,
    qpos_ref,
    kspan_ref,
    kpos_ref,
    table_ref,
    res_ref,
    wo_ref,
    gain_ref,
    wg_ref,
    wu_ref,
    wd_ref,
    att_out,
    mix_out,
    kv,
    q3,
    m_s,
    l_s,
    acc_s,
    att,
    wo2,
    wd2,
    wg2,
    wu2,
    res2,
    gain2,
    res_s,
    part,
    half_in,
    full_in,
    z_out,
    z_in,
    total_s,
    stream,
    sq_out,
    sq_in,
    normed,
    gu,
    gu_half,
    gu_full,
    gu_z,
    hid,
    part2,
    half_in2,
    full_in2,
    z_out2,
    z_in2,
    total_s2,
    mixed_s,
    mix_t,
    mix_recv,
    send_sem,
    recv_sem,
    local_sem,
):
    c = lax.axis_index("context")
    t = lax.axis_index("tensor")
    y, z, k = c // 4, lax.rem(c // 2, 2), lax.rem(c, 2)
    zl, x = t // 4, lax.rem(t, 4)
    yp, ym, yo = lax.rem(y + 1, 4), lax.rem(y + 3, 4), lax.rem(y + 2, 4)
    xp, xm = lax.rem(x + 1, 4), lax.rem(x + 3, 4)
    zo, ko = 1 - z, 1 - k

    def dev(y_=None, z_=None, k_=None, zl_=None, x_=None):
        y_ = y if y_ is None else y_
        z_ = z if z_ is None else z_
        k_ = k if k_ is None else k_
        zl_ = zl if zl_ is None else zl_
        x_ = x if x_ is None else x_
        return (4 * y_ + 2 * z_ + k_, 4 * zl_ + x_)

    sibling, across = dev(k_=ko), dev(z_=zo)
    up_y, down_y = dev(y_=yp), dev(y_=ym)
    up_x, down_x = dev(x_=xp), dev(x_=xm)
    zl_peers = [dev(zl_=lax.rem(zl + d, 4)) for d in (1, 2, 3)]
    norm_peers = [
        dev(y_=lax.rem(y + dy, 4), z_=lax.rem(z + dz, 2))
        for dy in range(4)
        for dz in range(2)
        if dy or dz
    ]
    is_home = lax.rem(x + k, 2) == 0
    is_relay = lax.rem(x + k, 2) == 1

    count = [0]
    sent = []

    def numbers(*shape):
        base = count[0]
        count[0] += math.prod(shape)

        def at(*index):
            flat = 0
            for size, one in zip(shape, index):
                flat = flat * size + one
            return base + flat

        return at

    def copy(src, dst, to, number):
        return pltpu.make_async_remote_copy(
            src_ref=src,
            dst_ref=dst,
            send_sem=send_sem.at[number],
            recv_sem=recv_sem.at[number],
            device_id=to,
            device_id_type=MESH,
        )

    def send(src, dst, to, number):
        one = copy(src, dst, to, number)
        one.start()
        sent.append(one)

    def arrived(dst, number):
        copy(dst, dst, sibling, number).wait_recv()

    kv_head = t // 2
    head_columns = pl.ds(pl.multiple_of(kv_head * DH, DH), DH)
    my_rows = pl.ds(pl.multiple_of(k * COLS, COLS), COLS)
    loads = [
        pltpu.make_async_copy(key_ref.at[:, head_columns], kv.at[c, :, 0:DH], local_sem.at[0]),
        pltpu.make_async_copy(
            value_ref.at[:, head_columns], kv.at[c, :, DH : 2 * DH], local_sem.at[1]
        ),
        pltpu.make_async_copy(wo_ref, wo2.at[my_rows], local_sem.at[2]),
        pltpu.make_async_copy(res_ref, res2.at[my_rows], local_sem.at[3]),
        pltpu.make_async_copy(gain_ref, gain2.at[k], local_sem.at[4]),
        pltpu.make_async_copy(wg_ref, wg2.at[my_rows], local_sem.at[5]),
        pltpu.make_async_copy(wu_ref, wu2.at[my_rows], local_sem.at[6]),
        pltpu.make_async_copy(wd_ref, wd2.at[my_rows], local_sem.at[7]),
    ]
    for one in loads:
        one.start()

    barrier = pltpu.get_barrier_semaphore()
    peers = [sibling, up_x, down_x] + zl_peers + norm_peers
    for peer in peers:
        pl.semaphore_signal(barrier, inc=1, device_id=peer, device_id_type=MESH)
    pl.semaphore_wait(barrier, len(peers))

    loads[0].wait()
    loads[1].wait()
    kv_id = numbers(17)
    ids = [kv_id(n) for n in range(17)]

    def block_at(y_, z_, k_):
        return kv.at[4 * y_ + 2 * z_ + k_]

    def half_at(y_, z_, k_, h):
        return kv.at[4 * y_ + 2 * z_ + k_, h * (KROWS // 2) : (h + 1) * (KROWS // 2)]

    own = block_at(y, z, k)
    send(own, own, across, ids[0])
    send(own, own, up_y, ids[1])
    send(own, own, down_y, ids[2])
    send(own, own, sibling, ids[3])

    other = block_at(y, zo, k)
    arrived(other, ids[0])
    send(other, other, up_y, ids[4])
    send(other, other, down_y, ids[5])
    send(other, other, sibling, ids[6])
    b = block_at(ym, z, k)
    arrived(b, ids[1])
    send(half_at(ym, z, k, 0), half_at(ym, z, k, 0), up_y, ids[7])
    send(b, b, sibling, ids[9])
    b = block_at(yp, z, k)
    arrived(b, ids[2])
    send(half_at(yp, z, k, 1), half_at(yp, z, k, 1), down_y, ids[8])
    send(b, b, sibling, ids[10])
    b = block_at(ym, zo, k)
    arrived(b, ids[4])
    send(half_at(ym, zo, k, 0), half_at(ym, zo, k, 0), up_y, ids[11])
    send(b, b, sibling, ids[13])
    b = block_at(yp, zo, k)
    arrived(b, ids[5])
    send(half_at(yp, zo, k, 1), half_at(yp, zo, k, 1), down_y, ids[12])
    send(b, b, sibling, ids[14])

    for one in loads[2:]:
        one.wait()
    weight_id = numbers(6)
    half_rows = pl.ds(pl.multiple_of(k * COLS, COLS), COLS)
    other_rows = pl.ds(pl.multiple_of(ko * COLS, COLS), COLS)
    joint = (wo2, res2, wg2, wu2, wd2)
    for n, weights in enumerate(joint):
        send(weights.at[half_rows], weights.at[half_rows], sibling, weight_id(n))
    send(gain2.at[k], gain2.at[k], sibling, weight_id(5))

    for h in range(NH):
        q3[h] = q_ref[:, h * DH : (h + 1) * DH]
    m_s[...] = jnp.full(m_s.shape, BLOCKED, F32)
    l_s[...] = jnp.zeros(l_s.shape, F32)
    acc_s[...] = jnp.zeros(acc_s.shape, F32)

    def as_column(row):
        return jnp.broadcast_to(row.astype(F32), (ROWS, ROWS)).T.astype(jnp.int32)

    q_span = as_column(qspan_ref[pl.ds(c, 1), :])
    q_pos = as_column(qpos_ref[pl.ds(c, 1), :])

    def attend(group):
        visible = []
        for n in range(8):
            tile = 8 * group + n
            allowed = table_ref[c, tile] == 1
            spans = jnp.where(allowed, kspan_ref[pl.ds(tile, 1), :], -1)
            places = kpos_ref[pl.ds(tile, 1), :]
            index = tile * TILE + lax.broadcasted_iota(jnp.int32, (1, TILE), 1)
            spans = jnp.broadcast_to(spans, (ROWS, TILE))
            places = jnp.broadcast_to(places, (ROWS, TILE))
            index = jnp.broadcast_to(index, (ROWS, TILE))
            visible.append(
                jnp.where(
                    ((spans == q_span) & (places < q_pos)) | (index < SINK), 0.0, BLOCKED
                ).astype(F32)
            )
        keys = kv[pl.ds(4 * group, 4)].reshape(4 * KROWS, 2 * DH)

        def one_head(h, carry):
            scores = lax.dot_general(
                q3[h], keys[:, :DH], (((1,), (1,)), ((), ())), preferred_element_type=F32
            )
            pieces = [
                jnp.where(
                    visible[n] == 0.0,
                    scores[:, n * TILE : (n + 1) * TILE] * SCORE_SCALE,
                    BLOCKED,
                )
                for n in range(8)
            ]
            best = pieces[0]
            for piece in pieces[1:]:
                best = jnp.maximum(best, piece)
            old = m_s[h]
            new = jnp.maximum(old, jnp.max(best, axis=1, keepdims=True))
            factor = jnp.exp2(old - new)
            weights = [jnp.exp2(piece - new) for piece in pieces]
            total = weights[0]
            for one in weights[1:]:
                total = total + one
            m_s[h] = new
            l_s[h] = l_s[h] * factor + total
            rounded = jnp.concatenate([one.astype(BF16) for one in weights], axis=1)
            acc_s[h] = acc_s[h] * factor + jnp.dot(
                rounded, keys[:, DH:], preferred_element_type=F32
            )
            return carry

        lax.fori_loop(0, NH, one_head, 0)

    arrived(block_at(y, z, ko), ids[3])
    arrived(block_at(y, zo, ko), ids[6])
    attend(y)

    arrived(half_at(yo, z, k, 0), ids[7])
    arrived(half_at(yo, z, k, 1), ids[8])
    b = block_at(yo, z, k)
    send(b, b, sibling, ids[15])
    arrived(half_at(yo, zo, k, 0), ids[11])
    arrived(half_at(yo, zo, k, 1), ids[12])
    b = block_at(yo, zo, k)
    send(b, b, sibling, ids[16])

    arrived(block_at(ym, z, ko), ids[9])
    arrived(block_at(ym, zo, ko), ids[13])
    attend(ym)
    arrived(block_at(yp, z, ko), ids[10])
    arrived(block_at(yp, zo, ko), ids[14])
    attend(yp)
    arrived(block_at(yo, z, ko), ids[15])
    arrived(block_at(yo, zo, ko), ids[16])
    attend(yo)

    mine = 2 * y + z
    for h in range(NH):
        total = jnp.sum(l_s[h], axis=1, keepdims=True)
        att[mine, :, h * DH : (h + 1) * DH] = (acc_s[h] / total).astype(BF16)

    def gather_context(whole, piece, id_at, ready):
        own = whole(y, z)
        send(own, own, across, id_at(0))
        send(own, own, up_y, id_at(1))
        send(own, own, down_y, id_at(2))
        ready(y, z)
        yield
        b = whole(y, zo)
        arrived(b, id_at(0))
        send(b, b, up_y, id_at(3))
        send(b, b, down_y, id_at(4))
        for zz, first, then in ((z, 1, 5), (zo, 3, 7)):
            arrived(whole(ym, zz), id_at(first))
            send(piece(ym, zz, 0), piece(ym, zz, 0), up_y, id_at(then))
            arrived(whole(yp, zz), id_at(first + 1))
            send(piece(yp, zz, 1), piece(yp, zz, 1), down_y, id_at(then + 1))
            if first == 1:
                ready(y, zo)
            ready(ym, zz)
            ready(yp, zz)
        for zz, then in ((z, 5), (zo, 7)):
            arrived(piece(yo, zz, 0), id_at(then))
            arrived(piece(yo, zz, 1), id_at(then + 1))
            ready(yo, zz)

    def lagged(lag, work):
        waiting = []

        def add(*one):
            waiting.append(one)
            if len(waiting) > lag:
                work(*waiting.pop(0))

        def flush():
            while waiting:
                work(*waiting.pop(0))

        return add, flush

    home_j = x // 2
    plus_j, minus_j = xp // 2, xm // 2
    order = [(d, lax.rem(zl + d, 4)) for d in (2, 1, 3, 0)]

    class Scatter:
        def __init__(self, shares, halves, fulls, out, inn, total):
            self.shares, self.halves, self.fulls = shares, halves, fulls
            self.out, self.inn, self.total = out, inn, total
            self.half_id = numbers(2, 4, 2)
            self.full_id = numbers(2, 4, 2)
            self.z_id = numbers(2, 3)

        def half(self, h, to, way):
            rows = slice(way * QUARTER, (way + 1) * QUARTER)
            return copy(
                self.shares.at[h, 2 * to + 1 - home_j, rows],
                self.halves.at[h, way, to],
                (up_x, down_x)[way],
                self.half_id(h, to, way),
            )

        def full(self, h, to, way):
            return copy(
                self.shares.at[h, 2 * to + (plus_j, minus_j)[way]],
                self.fulls.at[h, way, to],
                (up_x, down_x)[way],
                self.full_id(h, to, way),
            )

        def along_z(self, h, d):
            return copy(
                self.out.at[h, d - 1], self.inn.at[h, d - 1], zl_peers[d - 1], self.z_id(h, d - 1)
            )

        def ready(self, h, to, j):
            @pl.when(is_home & (j == 1 - home_j))
            def _():
                self.half(h, to, 0).start()
                self.half(h, to, 1).start()

        def relay(self, h, to, j):
            for way, at in ((0, plus_j), (1, minus_j)):
                rows = slice(way * QUARTER, (way + 1) * QUARTER)

                @pl.when(is_relay & (j == at))
                def _():
                    i = 2 * to + at
                    arrived(self.halves.at[h, way, to], self.half_id(h, to, way))
                    self.shares[h, i, rows] = (
                        self.shares[h, i, rows].astype(F32) + self.halves[h, way, to].astype(F32)
                    ).astype(BF16)
                    self.full(h, to, way).start()

        def finish_x(self, h):
            for d, to in order:
                arrived(self.fulls.at[h, 0, to], self.full_id(h, to, 0))
                arrived(self.fulls.at[h, 1, to], self.full_id(h, to, 1))
                here = (
                    self.shares[h, 2 * to + home_j].astype(F32)
                    + self.fulls[h, 0, to].astype(F32)
                    + self.fulls[h, 1, to].astype(F32)
                )
                if d:
                    self.out[h, d - 1] = here.astype(BF16)
                    self.along_z(h, d).start()
                else:
                    self.total[h] = here

        def finish_z(self, h):
            total = self.total[h]
            for d in (1, 3, 2):
                arrived(self.inn.at[h, d - 1], self.z_id(h, d - 1))
                total = total + self.inn[h, d - 1].astype(F32)
            return total

        def wait_sends(self):
            @pl.when(is_home)
            def _():
                for h in range(2):
                    for d in range(4):
                        self.half(h, d, 0).wait_send()
                        self.half(h, d, 1).wait_send()
                    for d in (1, 2, 3):
                        self.along_z(h, d).wait_send()

            @pl.when(is_relay)
            def _():
                for h in range(2):
                    for d in range(4):
                        self.full(h, d, 0).wait_send()
                        self.full(h, d, 1).wait_send()

    projected = Scatter(part, half_in, full_in, z_out, z_in, total_s)
    arrived(wo2.at[other_rows], weight_id(0))
    seen = []
    relay_a, flush_a = lagged(2, lambda to, j: projected.relay(0, to, j))

    def project(to, j):
        i = 2 * to + j
        rows = lax.dot_general(
            att[i], wo2[...], (((1,), (1,)), ((), ())), preferred_element_type=F32
        ).astype(BF16)
        part[0, i] = rows[:HALF]
        part[1, i] = rows[HALF:]
        projected.ready(0, to, j)
        seen.append((to, j))
        relay_a(to, j)

    for _ in gather_context(
        lambda y_, z_: att.at[2 * y_ + z_],
        lambda y_, z_, h: att.at[2 * y_ + z_, h * HALF : (h + 1) * HALF],
        numbers(9),
        project,
    ):
        pass
    for to, j in seen:
        projected.ready(1, to, j)
    flush_a()
    for to, j in seen:
        projected.relay(1, to, j)
    att_out[...] = att[mine]

    norm_id = numbers(2, 7)
    gather_z_id = numbers(2, 3)
    gather_x_id = numbers(2, 4, 2)
    gather_half_id = numbers(2, 4, 2)
    arrived(res2.at[other_rows], weight_id(1))
    arrived(gain2.at[ko], weight_id(5))

    def square(h, n):
        return copy(sq_out.at[h], sq_in.at[h, n], norm_peers[n], norm_id(h, n))

    def gather_z(h, d):
        own = normed.at[h, 2 * zl + home_j]
        return copy(own, own, zl_peers[d - 1], gather_z_id(h, d - 1))

    def gather_x(h, zq, way):
        b = normed.at[h, 2 * zq + home_j]
        return copy(b, b, (up_x, down_x)[way], gather_x_id(h, zq, way))

    def gather_half(h, zq, way):
        j = (minus_j, plus_j)[way]
        b = normed.at[h, 2 * zq + j, way * QUARTER : (way + 1) * QUARTER]
        return copy(b, b, (up_x, down_x)[way], gather_half_id(h, zq, way))

    def sum_squares(h):
        total = projected.finish_z(h)
        rounded = (res_s[h] + total).astype(BF16)
        stream[h] = rounded
        st = rounded.astype(F32)
        squares = jnp.sum(st * st, axis=1, keepdims=True)
        squares = jnp.concatenate([squares, squares], axis=0)
        sq_out[h] = jnp.broadcast_to(squares, (ROWS, ROWS)).T[0:8]
        for n in range(7):
            square(h, n).start()

    def normalise(h):
        whole = sq_out[h]
        for n in range(7):
            arrived(sq_in.at[h, n], norm_id(h, n))
            whole = whole + sq_in[h, n]
        column = jnp.broadcast_to(whole[0:1], (ROWS, ROWS)).T[0:HALF, 0:1]
        gain = jnp.concatenate([gain2[0][0:1], gain2[1][0:1]], axis=1)
        st = stream[h].astype(F32)
        normed[h, 2 * zl + home_j] = (st * lax.rsqrt(column / D + 1e-05) * gain).astype(BF16)
        for way in range(2):
            gather_x(h, zl, way).start()
        for d in (2, 1, 3):
            gather_z(h, d).start()

    @pl.when(is_home)
    def _():
        rows = res2[...].astype(F32).T
        res_s[0] = rows[:HALF]
        res_s[1] = rows[HALF:]
        projected.finish_x(0)
        sum_squares(0)
        projected.finish_x(1)
        normalise(0)

    arrived(wg2.at[other_rows], weight_id(2))
    arrived(wu2.at[other_rows], weight_id(3))
    half_id = numbers(2, 2, 2)
    full_id = numbers(2, 2, 2)
    cross_id = numbers(2)
    first_j = jnp.where(is_home, home_j, minus_j)

    def y_half(h, zz, way):
        rows = slice(way * QUARTER, (way + 1) * QUARTER)
        return copy(
            gu.at[h, 2 * yo + zz, :, rows],
            gu_half.at[h, way, zz],
            (up_y, down_y)[way],
            half_id(h, zz, way),
        )

    def y_full(h, zz, way):
        return copy(
            gu.at[h, 2 * (yp, ym)[way] + zz],
            gu_full.at[h, way, zz],
            (up_y, down_y)[way],
            full_id(h, zz, way),
        )

    def y_cross(h):
        return copy(gu.at[h, 2 * y + zo], gu_z.at[h], across, cross_id(h))

    def gate_up(h, zq, j):
        i = 2 * zq + j
        rows = normed[h, i]
        gu[h, i, 0] = jnp.dot(rows, wg2[...], preferred_element_type=F32).astype(BF16)
        gu[h, i, 1] = jnp.dot(rows, wu2[...], preferred_element_type=F32).astype(BF16)

        @pl.when(lax.rem(zq - y + 4, 4) == 2)
        def _():
            y_half(h, j, 0).start()
            y_half(h, j, 1).start()

    def steps_back(n):
        d = jnp.where(n < 2, n, 5 - n)
        return d, lax.rem(zl + 4 - d, 4)

    def take_first(h, n):
        d, zq = steps_back(n)

        @pl.when(is_home & (n > 0))
        def _():
            arrived(normed.at[h, 2 * zq + home_j], gather_z_id(h, d - 1))
            gather_x(h, zq, 0).start()
            gather_x(h, zq, 1).start()

        @pl.when(is_relay)
        def _():
            arrived(normed.at[h, 2 * zq + minus_j], gather_x_id(h, zq, 0))
            gather_half(h, zq, 0).start()
            arrived(normed.at[h, 2 * zq + plus_j], gather_x_id(h, zq, 1))
            gather_half(h, zq, 1).start()

        gate_up(h, zq, first_j)

    def take_second(h, n):
        d, zq = steps_back(n)

        @pl.when(is_home)
        def _():
            for way in range(2):
                b = normed.at[h, 2 * zq + 1 - home_j, way * QUARTER : (way + 1) * QUARTER]
                arrived(b, gather_half_id(h, zq, way))

        gate_up(h, zq, 1 - first_j)

    def y_relay(h, n):
        d, zq = steps_back(n)
        for way, there in ((0, yp), (1, ym)):
            rows = slice(way * QUARTER, (way + 1) * QUARTER)

            @pl.when(zq == there)
            def _():
                for zz in range(2):
                    i = 2 * there + zz
                    arrived(gu_half.at[h, way, zz], half_id(h, zz, way))
                    gu[h, i, :, rows] = (
                        gu[h, i, :, rows].astype(F32) + gu_half[h, way, zz].astype(F32)
                    ).astype(BF16)
                    y_full(h, zz, way).start()

    def own_sum(h, zz, which):
        return (
            gu[h, 2 * y + zz, which].astype(F32)
            + gu_full[h, 0, zz, which].astype(F32)
            + gu_full[h, 1, zz, which].astype(F32)
        )

    def finish_y_across(h):
        arrived(gu_full.at[h, 0, zo], full_id(h, zo, 0))
        arrived(gu_full.at[h, 1, zo], full_id(h, zo, 1))
        for which in range(2):
            gu[h, 2 * y + zo, which] = own_sum(h, zo, which).astype(BF16)
        y_cross(h).start()

    def finish_y(h):
        arrived(gu_full.at[h, 0, z], full_id(h, z, 0))
        arrived(gu_full.at[h, 1, z], full_id(h, z, 1))
        arrived(gu_z.at[h], cross_id(h))
        gate = own_sum(h, z, 0) + gu_z[h, 0].astype(F32)
        up = own_sum(h, z, 1) + gu_z[h, 1].astype(F32)
        hid[h, mine] = (gate / (1.0 + jnp.exp(-gate)) * up).astype(BF16)

    def steps_a(n, carry):
        @pl.when(n < 4)
        def _():
            take_first(0, n)

        @pl.when(is_home & (n == 1))
        def _():
            sum_squares(1)

        @pl.when(is_home & (n == 2))
        def _():
            normalise(1)

        @pl.when((n >= 1) & (n < 5))
        def _():
            take_second(0, n - 1)

        @pl.when(n >= 2)
        def _():
            y_relay(0, n - 2)

        return carry

    def steps_b(n, carry):
        @pl.when(n < 4)
        def _():
            take_first(1, n)

        @pl.when(n >= 1)
        def _():
            take_second(1, n - 1)

        return carry

    lax.fori_loop(0, 6, steps_a, 0)
    lax.fori_loop(0, 5, steps_b, 0)
    finish_y_across(0)
    for n in range(4):
        y_relay(1, n)

    arrived(wd2.at[other_rows], weight_id(4))
    summed = Scatter(part2, half_in2, full_in2, z_out2, z_in2, total_s2)

    def spread_hidden(h):
        relay, flush = lagged(2, lambda to, j: summed.relay(h, to, j))

        def down(to, j):
            i = 2 * to + j
            part2[h, i] = lax.dot_general(
                hid[h, i], wd2[...], (((1,), (1,)), ((), ())), preferred_element_type=F32
            ).astype(BF16)
            summed.ready(h, to, j)
            relay(to, j)

        yield from gather_context(
            lambda y_, z_: hid.at[h, 2 * y_ + z_],
            lambda y_, z_, q: hid.at[h, 2 * y_ + z_, q * QUARTER : (q + 1) * QUARTER],
            numbers(9),
            down,
        )
        flush()

    finish_y(0)
    spread_a, spread_b = spread_hidden(0), spread_hidden(1)
    next(spread_a)
    finish_y_across(1)
    for _ in spread_a:
        pass
    finish_y(1)
    next(spread_b)

    @pl.when(is_home)
    def _():
        summed.finish_x(0)

    for _ in spread_b:
        pass

    mix_id = numbers(1)(0)
    mix_mine = mix_t.at[other_rows]

    @pl.when(is_home)
    def _():
        mixed_s[0] = stream[0].astype(F32) + summed.finish_z(0)
        summed.finish_x(1)
        mixed_s[1] = stream[1].astype(F32) + summed.finish_z(1)
        mixed = jnp.concatenate([mixed_s[0], mixed_s[1]], axis=0)
        mix_t[...] = mixed.T.astype(BF16)
        copy(mix_mine, mix_recv, sibling, mix_id).start()
        mix_out[...] = mix_t[half_rows]
        copy(mix_mine, mix_recv, sibling, mix_id).wait_send()

    @pl.when(is_relay)
    def _():
        arrived(mix_recv, mix_id)
        mix_out[...] = mix_recv[...]

    for one in sent:
        one.wait_send()
    projected.wait_sends()
    summed.wait_sends()
    for h in range(2):
        for zz in range(2):
            for way in range(2):
                y_half(h, zz, way).wait_send()
                y_full(h, zz, way).wait_send()
        y_cross(h).wait_send()

    @pl.when(is_home)
    def _():
        for h in range(2):
            for n in range(7):
                square(h, n).wait_send()
            for d in (1, 2, 3):
                gather_z(h, d).wait_send()
            for zq in range(4):
                for way in range(2):
                    gather_x(h, zq, way).wait_send()

    @pl.when(is_relay)
    def _():
        for h in range(2):
            for zq in range(4):
                for way in range(2):
                    gather_half(h, zq, way).wait_send()

    assert count[0] <= N_COPIES


def local(
    queries,
    context_keys,
    context_values,
    query_span,
    query_position,
    key_span,
    key_position,
    tile_table,
    residual,
    out_weight,
    norm_gain,
    gate_weight,
    up_weight,
    down_weight,
):
    vmem = pl.BlockSpec(memory_space=pltpu.VMEM)
    smem = pl.BlockSpec(memory_space=pltpu.SMEM)
    hbm = pl.BlockSpec(memory_space=pl.ANY)
    gain = jnp.broadcast_to(norm_gain.astype(F32)[None, :], (8, COLS))
    def stages():
        return [
            pltpu.VMEM((2, BLOCKS, HALF, CC), BF16),
            pltpu.VMEM((2, 2, 4, QUARTER, CC), BF16),
            pltpu.VMEM((2, 2, 4, HALF, CC), BF16),
            pltpu.VMEM((2, 3, HALF, CC), BF16),
            pltpu.VMEM((2, 3, HALF, CC), BF16),
            pltpu.VMEM((2, HALF, CC), F32),
        ]

    scratch = [
        pltpu.VMEM((16, KROWS, 2 * DH), BF16),
        pltpu.VMEM((NH, ROWS, DH), BF16),
        pltpu.VMEM((NH, ROWS, DH), F32),
        pltpu.VMEM((NH, ROWS, DH), F32),
        pltpu.VMEM((NH, ROWS, DH), F32),
        pltpu.VMEM((BLOCKS, ROWS, NH * DH), BF16),
        pltpu.VMEM((CC, NH * DH), BF16),
        pltpu.VMEM((CC, FF), BF16),
        pltpu.VMEM((CC, FF), BF16),
        pltpu.VMEM((CC, FF), BF16),
        pltpu.VMEM((CC, ROWS), BF16),
        pltpu.VMEM((2, 8, COLS), F32),
        pltpu.VMEM((2, HALF, CC), F32),
        *stages(),
        pltpu.VMEM((2, HALF, CC), BF16),
        pltpu.VMEM((2, 8, ROWS), F32),
        pltpu.VMEM((2, 7, 8, ROWS), F32),
        pltpu.VMEM((2, BLOCKS, HALF, CC), BF16),
        pltpu.VMEM((2, BLOCKS, 2, HALF, FF), BF16),
        pltpu.VMEM((2, 2, 2, 2, QUARTER, FF), BF16),
        pltpu.VMEM((2, 2, 2, 2, HALF, FF), BF16),
        pltpu.VMEM((2, 2, HALF, FF), BF16),
        pltpu.VMEM((2, BLOCKS, HALF, FF), BF16),
        *stages(),
        pltpu.VMEM((2, HALF, CC), F32),
        pltpu.VMEM((CC, ROWS), BF16),
        pltpu.VMEM((COLS, ROWS), BF16),
        pltpu.SemaphoreType.DMA((N_COPIES,)),
        pltpu.SemaphoreType.DMA((N_COPIES,)),
        pltpu.SemaphoreType.DMA((8,)),
    ]
    attention, mixed = pl.pallas_call(
        layer_kernel,
        out_shape=(
            jax.ShapeDtypeStruct(queries.shape, BF16),
            jax.ShapeDtypeStruct(residual.shape[::-1], BF16),
        ),
        in_specs=[vmem, hbm, hbm, vmem, vmem, vmem, vmem, smem, hbm, hbm, hbm, hbm, hbm, hbm],
        out_specs=(vmem, vmem),
        scratch_shapes=scratch,
        compiler_params=pltpu.CompilerParams(
            collective_id=0, has_side_effects=True, vmem_limit_bytes=60 * 2**20
        ),
        cost_estimate=pl.CostEstimate(
            flops=9_000_000_000, bytes_accessed=8_000_000, transcendentals=2_000_000
        ),
        name="layer",
    )(
        queries,
        context_keys,
        context_values,
        query_span.reshape(16, TILE),
        query_position.reshape(16, TILE),
        key_span.reshape(32, TILE),
        key_position.reshape(32, TILE),
        tile_table,
        residual.T,
        out_weight.T,
        gain,
        gate_weight,
        up_weight,
        down_weight.T,
    )
    return attention, mixed.T


def solution(mesh):
    placed = (
        P("context", "tensor"),
        P("context", None),
        P("context", None),
        P(),
        P(),
        P(),
        P(),
        P(),
        P("tensor", "context"),
        P("tensor", "context"),
        P("context"),
        P("context", "tensor"),
        P("context", "tensor"),
        P("tensor", "context"),
    )
    return jax.shard_map(
        local,
        mesh=mesh,
        in_specs=placed,
        out_specs=(P("context", "tensor"), P("tensor", "context")),
        check_vma=False,
    )
```

```python
import math

import jax
import jax.numpy as jnp
from jax import lax
from jax.experimental import pallas as pl
from jax.experimental.pallas import tpu as pltpu
from jax.sharding import PartitionSpec as P

MESH = pl.DeviceIdType.MESH
F32 = jnp.float32
BF16 = jnp.bfloat16

D = 7168
DH = 128
TILE = 128
SINK = 4
ROWS = 128
HALF = ROWS // 2
QUARTER = HALF // 2
NH = 3
KROWS = 256
COLS = 448
CC = 2 * COLS
FF = 1200
WIDE = 1280
BLOCKS = 8

BLOCKED = -1e30
SCORE_SCALE = math.log2(math.e) / math.sqrt(DH)

N_COPIES = 260


def layer_kernel(
    q_ref,
    key_ref,
    value_ref,
    qspan_ref,
    qpos_ref,
    kspan_ref,
    kpos_ref,
    table_ref,
    res_ref,
    wo_ref,
    gain_ref,
    wg_ref,
    wu_ref,
    wd_ref,
    att_out,
    mix_out,
    kv,
    q3,
    m_s,
    l_s,
    acc_s,
    att,
    wo2,
    wd2,
    wg2,
    wu2,
    res2,
    res_s,
    part,
    half_in,
    full_in,
    z_out,
    z_in,
    total_s,
    normed,
    gu,
    gu_half,
    gu_full,
    gu_z,
    hid,
    part2,
    half_in2,
    full_in2,
    z_out2,
    z_in2,
    total_s2,
    wd_t,
    mixed_s,
    mix_t,
    mix_recv,
    send_sem,
    recv_sem,
    local_sem,
):
    c = lax.axis_index("context")
    t = lax.axis_index("tensor")
    y, z, k = c // 4, lax.rem(c // 2, 2), lax.rem(c, 2)
    zl, x = t // 4, lax.rem(t, 4)
    yp, ym, yo = lax.rem(y + 1, 4), lax.rem(y + 3, 4), lax.rem(y + 2, 4)
    xp, xm = lax.rem(x + 1, 4), lax.rem(x + 3, 4)
    zo, ko = 1 - z, 1 - k

    def dev(y_=None, z_=None, k_=None, zl_=None, x_=None):
        y_ = y if y_ is None else y_
        z_ = z if z_ is None else z_
        k_ = k if k_ is None else k_
        zl_ = zl if zl_ is None else zl_
        x_ = x if x_ is None else x_
        return (4 * y_ + 2 * z_ + k_, 4 * zl_ + x_)

    sibling, across = dev(k_=ko), dev(z_=zo)
    up_y, down_y = dev(y_=yp), dev(y_=ym)
    up_x, down_x = dev(x_=xp), dev(x_=xm)
    zl_peers = [dev(zl_=lax.rem(zl + d, 4)) for d in (1, 2, 3)]
    is_home = lax.rem(x + k, 2) == 0
    is_relay = lax.rem(x + k, 2) == 1

    count = [0]
    sent = []

    def numbers(*shape):
        base = count[0]
        count[0] += math.prod(shape)

        def at(*index):
            flat = 0
            for size, one in zip(shape, index):
                flat = flat * size + one
            return base + flat

        return at

    def copy(src, dst, to, number):
        return pltpu.make_async_remote_copy(
            src_ref=src,
            dst_ref=dst,
            send_sem=send_sem.at[number],
            recv_sem=recv_sem.at[number],
            device_id=to,
            device_id_type=MESH,
        )

    def send(src, dst, to, number):
        one = copy(src, dst, to, number)
        one.start()
        sent.append(one)

    def arrived(dst, number):
        copy(dst, dst, sibling, number).wait_recv()

    kv_head = t // 2
    head_columns = pl.ds(pl.multiple_of(kv_head * DH, DH), DH)
    my_rows = pl.ds(pl.multiple_of(k * COLS, COLS), COLS)
    loads = [
        pltpu.make_async_copy(key_ref.at[:, head_columns], kv.at[c, :, 0:DH], local_sem.at[0]),
        pltpu.make_async_copy(
            value_ref.at[:, head_columns], kv.at[c, :, DH : 2 * DH], local_sem.at[1]
        ),
        pltpu.make_async_copy(wo_ref, wo2.at[my_rows], local_sem.at[2]),
        pltpu.make_async_copy(res_ref, res2.at[my_rows], local_sem.at[3]),
        pltpu.make_async_copy(wg_ref, wg2.at[my_rows], local_sem.at[4]),
        pltpu.make_async_copy(wu_ref, wu2.at[my_rows], local_sem.at[5]),
        pltpu.make_async_copy(wd_ref, wd2.at[my_rows], local_sem.at[6]),
    ]
    for one in loads:
        one.start()

    barrier = pltpu.get_barrier_semaphore()
    peers = [sibling, across, up_y, down_y, up_x, down_x] + zl_peers
    for peer in peers:
        pl.semaphore_signal(barrier, inc=1, device_id=peer, device_id_type=MESH)
    pl.semaphore_wait(barrier, len(peers))

    loads[0].wait()
    loads[1].wait()
    kv_id = numbers(17)
    ids = [kv_id(n) for n in range(17)]

    def block_at(y_, z_, k_):
        return kv.at[4 * y_ + 2 * z_ + k_]

    def half_at(y_, z_, k_, h):
        return kv.at[4 * y_ + 2 * z_ + k_, h * (KROWS // 2) : (h + 1) * (KROWS // 2)]

    own = block_at(y, z, k)
    send(own, own, across, ids[0])
    send(own, own, up_y, ids[1])
    send(own, own, down_y, ids[2])
    send(own, own, sibling, ids[3])

    for one in loads[2:]:
        one.wait()
    gain = jnp.broadcast_to(gain_ref[0:1, :], (DH, COLS)).T[:, 0:1]
    for weights in (wg2, wu2):
        weights[my_rows] = (weights[my_rows].astype(F32) * gain).astype(BF16)

    other = block_at(y, zo, k)
    arrived(other, ids[0])
    send(other, other, up_y, ids[4])
    send(other, other, down_y, ids[5])
    send(other, other, sibling, ids[6])
    b = block_at(ym, z, k)
    arrived(b, ids[1])
    send(half_at(ym, z, k, 0), half_at(ym, z, k, 0), up_y, ids[7])
    send(b, b, sibling, ids[9])
    b = block_at(yp, z, k)
    arrived(b, ids[2])
    send(half_at(yp, z, k, 1), half_at(yp, z, k, 1), down_y, ids[8])
    send(b, b, sibling, ids[10])
    b = block_at(ym, zo, k)
    arrived(b, ids[4])
    send(half_at(ym, zo, k, 0), half_at(ym, zo, k, 0), up_y, ids[11])
    send(b, b, sibling, ids[13])
    b = block_at(yp, zo, k)
    arrived(b, ids[5])
    send(half_at(yp, zo, k, 1), half_at(yp, zo, k, 1), down_y, ids[12])
    send(b, b, sibling, ids[14])

    weight_id = numbers(5)
    half_rows = pl.ds(pl.multiple_of(k * COLS, COLS), COLS)
    other_rows = pl.ds(pl.multiple_of(ko * COLS, COLS), COLS)
    joint = (wo2, res2, wg2, wu2, wd2)
    for n, weights in enumerate(joint):
        send(weights.at[half_rows], weights.at[half_rows], sibling, weight_id(n))

    for h in range(NH):
        q3[h] = q_ref[:, h * DH : (h + 1) * DH]
    m_s[...] = jnp.full(m_s.shape, BLOCKED, F32)
    l_s[...] = jnp.zeros(l_s.shape, F32)
    acc_s[...] = jnp.zeros(acc_s.shape, F32)

    def as_column(row):
        return jnp.broadcast_to(row.astype(F32), (ROWS, ROWS)).T.astype(jnp.int32)

    q_span = as_column(qspan_ref[pl.ds(c, 1), :])
    q_pos = as_column(qpos_ref[pl.ds(c, 1), :])

    def attend(group):
        visible = []
        for n in range(8):
            tile = 8 * group + n
            allowed = table_ref[c, tile] == 1
            spans = jnp.where(allowed, kspan_ref[pl.ds(tile, 1), :], -1)
            places = kpos_ref[pl.ds(tile, 1), :]
            index = tile * TILE + lax.broadcasted_iota(jnp.int32, (1, TILE), 1)
            spans = jnp.broadcast_to(spans, (ROWS, TILE))
            places = jnp.broadcast_to(places, (ROWS, TILE))
            index = jnp.broadcast_to(index, (ROWS, TILE))
            visible.append(
                jnp.where(
                    ((spans == q_span) & (places < q_pos)) | (index < SINK), 0.0, BLOCKED
                ).astype(F32)
            )
        keys = kv[pl.ds(4 * group, 4)].reshape(4 * KROWS, 2 * DH)

        def one_head(h, carry):
            scores = lax.dot_general(
                q3[h], keys[:, :DH], (((1,), (1,)), ((), ())), preferred_element_type=F32
            )
            pieces = [
                jnp.where(
                    visible[n] == 0.0,
                    scores[:, n * TILE : (n + 1) * TILE] * SCORE_SCALE,
                    BLOCKED,
                )
                for n in range(8)
            ]
            best = pieces[0]
            for piece in pieces[1:]:
                best = jnp.maximum(best, piece)
            old = m_s[h]
            new = jnp.maximum(old, jnp.max(best, axis=1, keepdims=True))
            factor = jnp.exp2(old - new)
            weights = [jnp.exp2(piece - new) for piece in pieces]
            total = weights[0]
            for one in weights[1:]:
                total = total + one
            m_s[h] = new
            l_s[h] = l_s[h] * factor + total
            rounded = jnp.concatenate([one.astype(BF16) for one in weights], axis=1)
            acc_s[h] = acc_s[h] * factor + jnp.dot(
                rounded, keys[:, DH:], preferred_element_type=F32
            )
            return carry

        lax.fori_loop(0, NH, one_head, 0)

    arrived(block_at(y, z, ko), ids[3])
    arrived(block_at(y, zo, ko), ids[6])
    attend(y)

    arrived(half_at(yo, z, k, 0), ids[7])
    arrived(half_at(yo, z, k, 1), ids[8])
    b = block_at(yo, z, k)
    send(b, b, sibling, ids[15])
    arrived(half_at(yo, zo, k, 0), ids[11])
    arrived(half_at(yo, zo, k, 1), ids[12])
    b = block_at(yo, zo, k)
    send(b, b, sibling, ids[16])

    arrived(block_at(ym, z, ko), ids[9])
    arrived(block_at(ym, zo, ko), ids[13])
    attend(ym)
    arrived(block_at(yp, z, ko), ids[10])
    arrived(block_at(yp, zo, ko), ids[14])
    attend(yp)
    arrived(block_at(yo, z, ko), ids[15])
    arrived(block_at(yo, zo, ko), ids[16])
    attend(yo)

    mine = 2 * y + z
    for h in range(NH):
        total = jnp.sum(l_s[h], axis=1, keepdims=True)
        att[mine, :, h * DH : (h + 1) * DH] = (acc_s[h] / total).astype(BF16)

    def gather_context(whole, piece, id_at, ready):
        own = whole(y, z)
        send(own, own, across, id_at(0))
        send(own, own, up_y, id_at(1))
        send(own, own, down_y, id_at(2))
        ready(y, z)
        yield
        b = whole(y, zo)
        arrived(b, id_at(0))
        send(b, b, up_y, id_at(3))
        send(b, b, down_y, id_at(4))
        for zz, first, then in ((z, 1, 5), (zo, 3, 7)):
            arrived(whole(ym, zz), id_at(first))
            send(piece(ym, zz, 0), piece(ym, zz, 0), up_y, id_at(then))
            arrived(whole(yp, zz), id_at(first + 1))
            send(piece(yp, zz, 1), piece(yp, zz, 1), down_y, id_at(then + 1))
            if first == 1:
                ready(y, zo)
            ready(ym, zz)
            ready(yp, zz)
        for zz, then in ((z, 5), (zo, 7)):
            arrived(piece(yo, zz, 0), id_at(then))
            arrived(piece(yo, zz, 1), id_at(then + 1))
            ready(yo, zz)

    def lagged(lag, work):
        waiting = []

        def add(*one):
            waiting.append(one)
            if len(waiting) > lag:
                work(*waiting.pop(0))

        def flush():
            while waiting:
                work(*waiting.pop(0))

        return add, flush

    home_j = x // 2
    plus_j, minus_j = xp // 2, xm // 2
    class Scatter:
        def __init__(self, shares, halves, fulls, out, inn, total):
            self.shares, self.halves, self.fulls = shares, halves, fulls
            self.out, self.inn, self.total = out, inn, total
            self.half_id = numbers(2, 4, 2)
            self.full_id = numbers(2, 4, 2)
            self.z_id = numbers(2, 4)

        def half(self, h, to, way):
            rows = slice(way * QUARTER, (way + 1) * QUARTER)
            return copy(
                self.shares.at[h, 2 * to + 1 - home_j, rows],
                self.halves.at[h, way, to],
                (up_x, down_x)[way],
                self.half_id(h, to, way),
            )

        def full(self, h, to, way):
            return copy(
                self.shares.at[h, 2 * to + (plus_j, minus_j)[way]],
                self.fulls.at[h, way, to],
                (up_x, down_x)[way],
                self.full_id(h, to, way),
            )

        def along_z(self, h, d):
            to = dev(zl_=lax.rem(zl + d, 4))
            return copy(self.out.at[h, d], self.inn.at[h, d], to, self.z_id(h, d))

        def ready(self, h, to, j):
            @pl.when(is_home & (j == 1 - home_j))
            def _():
                self.half(h, to, 0).start()
                self.half(h, to, 1).start()

        def relay(self, h, to, j):
            for way, at in ((0, plus_j), (1, minus_j)):
                rows = slice(way * QUARTER, (way + 1) * QUARTER)

                @pl.when(is_relay & (j == at))
                def _():
                    i = 2 * to + at
                    arrived(self.halves.at[h, way, to], self.half_id(h, to, way))
                    self.shares[h, i, rows] = (
                        self.shares[h, i, rows].astype(F32) + self.halves[h, way, to].astype(F32)
                    ).astype(BF16)
                    self.full(h, to, way).start()

        def finish_x(self, h):
            for to in (y, ym, yp, yo):
                arrived(self.fulls.at[h, 0, to], self.full_id(h, to, 0))
                arrived(self.fulls.at[h, 1, to], self.full_id(h, to, 1))
                here = (
                    self.shares[h, 2 * to + home_j].astype(F32)
                    + self.fulls[h, 0, to].astype(F32)
                    + self.fulls[h, 1, to].astype(F32)
                )

                @pl.when(to == zl)
                def _():
                    self.total[h] = here

                @pl.when(to != zl)
                def _():
                    d = lax.rem(to - zl + 4, 4)
                    self.out[h, d] = here.astype(BF16)
                    self.along_z(h, d).start()

        def finish_z(self, h):
            total = self.total[h]
            for d in (1, 3, 2):
                arrived(self.inn.at[h, d], self.z_id(h, d))
                total = total + self.inn[h, d].astype(F32)
            return total

        def wait_sends(self):
            @pl.when(is_home)
            def _():
                for h in range(2):
                    for d in range(4):
                        self.half(h, d, 0).wait_send()
                        self.half(h, d, 1).wait_send()
                    for d in (1, 2, 3):
                        self.along_z(h, d).wait_send()

            @pl.when(is_relay)
            def _():
                for h in range(2):
                    for d in range(4):
                        self.full(h, d, 0).wait_send()
                        self.full(h, d, 1).wait_send()

    projected = Scatter(part, half_in, full_in, z_out, z_in, total_s)
    arrived(wo2.at[other_rows], weight_id(0))
    seen = []
    relay_a, flush_a = lagged(2, lambda to, j: projected.relay(0, to, j))

    def project(to, j):
        i = 2 * to + j
        rows = lax.dot_general(
            att[i], wo2[...], (((1,), (1,)), ((), ())), preferred_element_type=F32
        ).astype(BF16)
        part[0, i] = rows[:HALF]
        part[1, i] = rows[HALF:]
        projected.ready(0, to, j)
        seen.append((to, j))
        relay_a(to, j)

    for _ in gather_context(
        lambda y_, z_: att.at[2 * y_ + z_],
        lambda y_, z_, h: att.at[2 * y_ + z_, h * HALF : (h + 1) * HALF],
        numbers(9),
        project,
    ):
        pass
    for to, j in seen:
        projected.ready(1, to, j)
    flush_a()
    for to, j in seen:
        projected.relay(1, to, j)
    att_out[...] = att[mine]

    gather_z_id = numbers(2, 3)
    gather_x_id = numbers(2, 4, 2)
    gather_half_id = numbers(2, 4, 2)
    arrived(res2.at[other_rows], weight_id(1))

    def gather_z(h, d):
        own = normed.at[h, 2 * zl + home_j]
        return copy(own, own, zl_peers[d - 1], gather_z_id(h, d - 1))

    def gather_x(h, zq, way):
        b = normed.at[h, 2 * zq + home_j]
        return copy(b, b, (up_x, down_x)[way], gather_x_id(h, zq, way))

    def gather_half(h, zq, way):
        j = (minus_j, plus_j)[way]
        b = normed.at[h, 2 * zq + j, way * QUARTER : (way + 1) * QUARTER]
        return copy(b, b, (up_x, down_x)[way], gather_half_id(h, zq, way))

    def make_stream(h):
        total = projected.finish_z(h)
        normed[h, 2 * zl + home_j] = (res_s[h] + total).astype(BF16)
        for way in range(2):
            gather_x(h, zl, way).start()
        for d in (2, 1, 3):
            gather_z(h, d).start()

    @pl.when(is_home)
    def _():
        rows = res2[...].astype(F32).T
        res_s[0] = rows[:HALF]
        res_s[1] = rows[HALF:]
        projected.finish_x(0)
        make_stream(0)
        projected.finish_x(1)

    arrived(wg2.at[other_rows], weight_id(2))
    arrived(wu2.at[other_rows], weight_id(3))
    half_id = numbers(2, 2, 2)
    full_id = numbers(2, 2, 2)
    cross_id = numbers(2)
    first_j = jnp.where(is_home, home_j, minus_j)

    def y_half(h, zz, way):
        rows = slice(way * QUARTER, (way + 1) * QUARTER)
        return copy(
            gu.at[h, 2 * yo + zz, :, rows],
            gu_half.at[h, way, zz],
            (up_y, down_y)[way],
            half_id(h, zz, way),
        )

    def y_full(h, zz, way):
        return copy(
            gu.at[h, 2 * (yp, ym)[way] + zz],
            gu_full.at[h, way, zz],
            (up_y, down_y)[way],
            full_id(h, zz, way),
        )

    def y_cross(h):
        return copy(gu.at[h, 2 * y + zo], gu_z.at[h], across, cross_id(h))

    def gate_up(h, zq, j):
        i = 2 * zq + j
        rows = normed[h, i]
        wide = rows.astype(F32)
        squares = jnp.broadcast_to(jnp.sum(wide * wide, axis=1, keepdims=True), (HALF, WIDE - FF))
        gate = jnp.dot(rows, wg2[...], preferred_element_type=F32)
        gu[h, i, 0] = jnp.concatenate([gate, squares], axis=1).astype(BF16)
        gu[h, i, 1, :, :FF] = jnp.dot(rows, wu2[...], preferred_element_type=F32).astype(BF16)

        @pl.when(lax.rem(zq - y + 4, 4) == 2)
        def _():
            y_half(h, j, 0).start()
            y_half(h, j, 1).start()

    def steps_back(n):
        d = jnp.where(n < 2, n, 5 - n)
        return d, lax.rem(zl + 4 - d, 4)

    def take_first(h, n):
        d, zq = steps_back(n)

        @pl.when(is_home & (n > 0))
        def _():
            arrived(normed.at[h, 2 * zq + home_j], gather_z_id(h, d - 1))
            gather_x(h, zq, 0).start()
            gather_x(h, zq, 1).start()

        @pl.when(is_relay)
        def _():
            arrived(normed.at[h, 2 * zq + minus_j], gather_x_id(h, zq, 0))
            gather_half(h, zq, 0).start()
            arrived(normed.at[h, 2 * zq + plus_j], gather_x_id(h, zq, 1))
            gather_half(h, zq, 1).start()

        gate_up(h, zq, first_j)

    def take_second(h, n):
        d, zq = steps_back(n)

        @pl.when(is_home)
        def _():
            for way in range(2):
                b = normed.at[h, 2 * zq + 1 - home_j, way * QUARTER : (way + 1) * QUARTER]
                arrived(b, gather_half_id(h, zq, way))

        gate_up(h, zq, 1 - first_j)

    def y_relay(h, n):
        d, zq = steps_back(n)
        for way, there in ((0, yp), (1, ym)):
            rows = slice(way * QUARTER, (way + 1) * QUARTER)

            @pl.when(zq == there)
            def _():
                for zz in (zo, z):
                    i = 2 * there + zz
                    arrived(gu_half.at[h, way, zz], half_id(h, zz, way))
                    gu[h, i, :, rows] = (
                        gu[h, i, :, rows].astype(F32) + gu_half[h, way, zz].astype(F32)
                    ).astype(BF16)
                    y_full(h, zz, way).start()

    def own_sum(h, zz, which):
        return (
            gu[h, 2 * y + zz, which].astype(F32)
            + gu_full[h, 0, zz, which].astype(F32)
            + gu_full[h, 1, zz, which].astype(F32)
        )

    def finish_y_across(h):
        arrived(gu_full.at[h, 0, zo], full_id(h, zo, 0))
        arrived(gu_full.at[h, 1, zo], full_id(h, zo, 1))
        for which in range(2):
            gu[h, 2 * y + zo, which] = own_sum(h, zo, which).astype(BF16)
        y_cross(h).start()

    def finish_y(h):
        arrived(gu_full.at[h, 0, z], full_id(h, z, 0))
        arrived(gu_full.at[h, 1, z], full_id(h, z, 1))
        arrived(gu_z.at[h], cross_id(h))
        gate = own_sum(h, z, 0) + gu_z[h, 0].astype(F32)
        up = (own_sum(h, z, 1) + gu_z[h, 1].astype(F32))[:, :FF]
        scale = lax.rsqrt(gate[:, FF : FF + 1] / D + 1e-05)
        gate, up = gate[:, :FF] * scale, up * scale
        hid[h, mine] = (gate / (1.0 + jnp.exp(-gate)) * up).astype(BF16)

    def steps_a(n, carry):
        @pl.when(n < 4)
        def _():
            take_first(0, n)

        @pl.when(is_home & (n == 1))
        def _():
            make_stream(1)

        @pl.when(n >= 1)
        def _():
            take_second(0, n - 1)

        @pl.when(n >= 3)
        def _():
            y_relay(0, n - 3)

        return carry

    def steps_b(n, carry):
        @pl.when(n < 4)
        def _():
            take_first(1, n)

        @pl.when(n < 2)
        def _():
            y_relay(0, n + 2)

        @pl.when(n >= 1)
        def _():
            take_second(1, n - 1)

        return carry

    lax.fori_loop(0, 5, steps_a, 0)
    lax.fori_loop(0, 5, steps_b, 0)
    arrived(wd2.at[other_rows], weight_id(4))
    wd_t[...] = wd2[...].T
    finish_y_across(0)
    for n in range(4):
        y_relay(1, n)

    summed = Scatter(part2, half_in2, full_in2, z_out2, z_in2, total_s2)

    def spread_hidden(h):
        relay, flush = lagged(2, lambda to, j: summed.relay(h, to, j))

        def down(to, j):
            i = 2 * to + j
            part2[h, i] = jnp.dot(hid[h, i], wd_t[...], preferred_element_type=F32).astype(BF16)
            summed.ready(h, to, j)
            relay(to, j)

        yield from gather_context(
            lambda y_, z_: hid.at[h, 2 * y_ + z_],
            lambda y_, z_, q: hid.at[h, 2 * y_ + z_, q * QUARTER : (q + 1) * QUARTER],
            numbers(9),
            down,
        )
        flush()

    finish_y(0)
    spread_a, spread_b = spread_hidden(0), spread_hidden(1)
    next(spread_a)
    finish_y_across(1)
    for _ in spread_a:
        pass
    finish_y(1)
    next(spread_b)

    @pl.when(is_home)
    def _():
        summed.finish_x(0)

    for _ in spread_b:
        pass

    mix_id = numbers(1)(0)
    mix_mine = mix_t.at[other_rows]

    @pl.when(is_home)
    def _():
        mixed_s[0] = normed[0, 2 * zl + home_j].astype(F32) + summed.finish_z(0)
        summed.finish_x(1)
        mixed_s[1] = normed[1, 2 * zl + home_j].astype(F32) + summed.finish_z(1)
        mixed = jnp.concatenate([mixed_s[0], mixed_s[1]], axis=0)
        mix_t[...] = mixed.T.astype(BF16)
        copy(mix_mine, mix_recv, sibling, mix_id).start()
        mix_out[...] = mix_t[half_rows]
        copy(mix_mine, mix_recv, sibling, mix_id).wait_send()

    @pl.when(is_relay)
    def _():
        arrived(mix_recv, mix_id)
        mix_out[...] = mix_recv[...]

    for one in sent:
        one.wait_send()
    projected.wait_sends()
    summed.wait_sends()
    for h in range(2):
        for zz in range(2):
            for way in range(2):
                y_half(h, zz, way).wait_send()
                y_full(h, zz, way).wait_send()
        y_cross(h).wait_send()

    @pl.when(is_home)
    def _():
        for h in range(2):
            for d in (1, 2, 3):
                gather_z(h, d).wait_send()
            for zq in range(4):
                for way in range(2):
                    gather_x(h, zq, way).wait_send()

    @pl.when(is_relay)
    def _():
        for h in range(2):
            for zq in range(4):
                for way in range(2):
                    gather_half(h, zq, way).wait_send()

    assert count[0] <= N_COPIES


def local(
    queries,
    context_keys,
    context_values,
    query_span,
    query_position,
    key_span,
    key_position,
    tile_table,
    residual,
    out_weight,
    norm_gain,
    gate_weight,
    up_weight,
    down_weight,
):
    vmem = pl.BlockSpec(memory_space=pltpu.VMEM)
    smem = pl.BlockSpec(memory_space=pltpu.SMEM)
    hbm = pl.BlockSpec(memory_space=pl.ANY)
    gain = jnp.broadcast_to(norm_gain.astype(F32)[None, :], (8, COLS))
    def stages():
        return [
            pltpu.VMEM((2, BLOCKS, HALF, CC), BF16),
            pltpu.VMEM((2, 2, 4, QUARTER, CC), BF16),
            pltpu.VMEM((2, 2, 4, HALF, CC), BF16),
            pltpu.VMEM((2, 4, HALF, CC), BF16),
            pltpu.VMEM((2, 4, HALF, CC), BF16),
            pltpu.VMEM((2, HALF, CC), F32),
        ]

    scratch = [
        pltpu.VMEM((16, KROWS, 2 * DH), BF16),
        pltpu.VMEM((NH, ROWS, DH), BF16),
        pltpu.VMEM((NH, ROWS, DH), F32),
        pltpu.VMEM((NH, ROWS, DH), F32),
        pltpu.VMEM((NH, ROWS, DH), F32),
        pltpu.VMEM((BLOCKS, ROWS, NH * DH), BF16),
        pltpu.VMEM((CC, NH * DH), BF16),
        pltpu.VMEM((CC, FF), BF16),
        pltpu.VMEM((CC, FF), BF16),
        pltpu.VMEM((CC, FF), BF16),
        pltpu.VMEM((CC, ROWS), BF16),
        pltpu.VMEM((2, HALF, CC), F32),
        *stages(),
        pltpu.VMEM((2, BLOCKS, HALF, CC), BF16),
        pltpu.VMEM((2, BLOCKS, 2, HALF, WIDE), BF16),
        pltpu.VMEM((2, 2, 2, 2, QUARTER, WIDE), BF16),
        pltpu.VMEM((2, 2, 2, 2, HALF, WIDE), BF16),
        pltpu.VMEM((2, 2, HALF, WIDE), BF16),
        pltpu.VMEM((2, BLOCKS, HALF, FF), BF16),
        *stages(),
        pltpu.VMEM((FF, CC), BF16),
        pltpu.VMEM((2, HALF, CC), F32),
        pltpu.VMEM((CC, ROWS), BF16),
        pltpu.VMEM((COLS, ROWS), BF16),
        pltpu.SemaphoreType.DMA((N_COPIES,)),
        pltpu.SemaphoreType.DMA((N_COPIES,)),
        pltpu.SemaphoreType.DMA((8,)),
    ]
    attention, mixed = pl.pallas_call(
        layer_kernel,
        out_shape=(
            jax.ShapeDtypeStruct(queries.shape, BF16),
            jax.ShapeDtypeStruct(residual.shape[::-1], BF16),
        ),
        in_specs=[vmem, hbm, hbm, vmem, vmem, vmem, vmem, smem, hbm, hbm, vmem, hbm, hbm, hbm],
        out_specs=(vmem, vmem),
        scratch_shapes=scratch,
        compiler_params=pltpu.CompilerParams(
            collective_id=0, has_side_effects=True, vmem_limit_bytes=60 * 2**20
        ),
        cost_estimate=pl.CostEstimate(
            flops=9_000_000_000, bytes_accessed=8_000_000, transcendentals=2_000_000
        ),
        name="layer",
    )(
        queries,
        context_keys,
        context_values,
        query_span.reshape(16, TILE),
        query_position.reshape(16, TILE),
        key_span.reshape(32, TILE),
        key_position.reshape(32, TILE),
        tile_table,
        residual.T,
        out_weight.T,
        gain,
        gate_weight,
        up_weight,
        down_weight.T,
    )
    return attention, mixed.T


def solution(mesh):
    placed = (
        P("context", "tensor"),
        P("context", None),
        P("context", None),
        P(),
        P(),
        P(),
        P(),
        P(),
        P("tensor", "context"),
        P("tensor", "context"),
        P("context"),
        P("context", "tensor"),
        P("context", "tensor"),
        P("tensor", "context"),
    )
    return jax.shard_map(
        local,
        mesh=mesh,
        in_specs=placed,
        out_specs=(P("context", "tensor"), P("tensor", "context")),
        check_vma=False,
    )
```

```python
import math

import jax
import jax.numpy as jnp
from jax import lax
from jax.experimental import pallas as pl
from jax.experimental.pallas import tpu as pltpu
from jax.sharding import PartitionSpec as P

MESH = pl.DeviceIdType.MESH
F32 = jnp.float32
BF16 = jnp.bfloat16

D = 7168
DH = 128
TILE = 128
SINK = 4
ROWS = 128
HALF = ROWS // 2
QUARTER = HALF // 2
NH = 3
KROWS = 256
COLS = 448
CC = 2 * COLS
FF = 1200
WIDE = 2432
BLOCKS = 8

BLOCKED = -1e30
SCORE_SCALE = math.log2(math.e) / math.sqrt(DH)

N_COPIES = 260


def layer_kernel(
    q_ref,
    key_ref,
    value_ref,
    qspan_ref,
    qpos_ref,
    kspan_ref,
    kpos_ref,
    table_ref,
    res_ref,
    wo_ref,
    gain_ref,
    wg_ref,
    wu_ref,
    wd_ref,
    att_out,
    mix_out,
    kv,
    q3,
    m_s,
    l_s,
    acc_s,
    att,
    wo2,
    wd2,
    wg2,
    wu2,
    res2,
    res_s,
    part,
    half_in,
    full_in,
    z_out,
    z_in,
    total_s,
    normed,
    gu,
    gu_half,
    gu_full,
    gu_z,
    hid,
    part2,
    half_in2,
    full_in2,
    z_out2,
    z_in2,
    total_s2,
    wd_t,
    mixed_s,
    mix_t,
    mix_recv,
    send_sem,
    recv_sem,
    local_sem,
):
    c = lax.axis_index("context")
    t = lax.axis_index("tensor")
    y, z, k = c // 4, lax.rem(c // 2, 2), lax.rem(c, 2)
    zl, x = t // 4, lax.rem(t, 4)
    yp, ym, yo = lax.rem(y + 1, 4), lax.rem(y + 3, 4), lax.rem(y + 2, 4)
    xp, xm = lax.rem(x + 1, 4), lax.rem(x + 3, 4)
    zo, ko = 1 - z, 1 - k

    def dev(y_=None, z_=None, k_=None, zl_=None, x_=None):
        y_ = y if y_ is None else y_
        z_ = z if z_ is None else z_
        k_ = k if k_ is None else k_
        zl_ = zl if zl_ is None else zl_
        x_ = x if x_ is None else x_
        return (4 * y_ + 2 * z_ + k_, 4 * zl_ + x_)

    sibling, across = dev(k_=ko), dev(z_=zo)
    up_y, down_y = dev(y_=yp), dev(y_=ym)
    up_x, down_x = dev(x_=xp), dev(x_=xm)
    zl_peers = [dev(zl_=lax.rem(zl + d, 4)) for d in (1, 2, 3)]
    is_home = lax.rem(x + k, 2) == 0
    is_relay = lax.rem(x + k, 2) == 1

    count = [0]
    sent = []

    def numbers(*shape):
        base = count[0]
        count[0] += math.prod(shape)

        def at(*index):
            flat = 0
            for size, one in zip(shape, index):
                flat = flat * size + one
            return base + flat

        return at

    def copy(src, dst, to, number):
        return pltpu.make_async_remote_copy(
            src_ref=src,
            dst_ref=dst,
            send_sem=send_sem.at[number],
            recv_sem=recv_sem.at[number],
            device_id=to,
            device_id_type=MESH,
        )

    def send(src, dst, to, number):
        one = copy(src, dst, to, number)
        one.start()
        sent.append(one)

    def arrived(dst, number):
        copy(dst, dst, sibling, number).wait_recv()

    kv_head = t // 2
    head_columns = pl.ds(pl.multiple_of(kv_head * DH, DH), DH)
    my_rows = pl.ds(pl.multiple_of(k * COLS, COLS), COLS)
    loads = [
        pltpu.make_async_copy(key_ref.at[:, head_columns], kv.at[c, :, 0:DH], local_sem.at[0]),
        pltpu.make_async_copy(
            value_ref.at[:, head_columns], kv.at[c, :, DH : 2 * DH], local_sem.at[1]
        ),
        pltpu.make_async_copy(wo_ref, wo2.at[my_rows], local_sem.at[2]),
        pltpu.make_async_copy(res_ref, res2.at[my_rows], local_sem.at[3]),
        pltpu.make_async_copy(wg_ref, wg2.at[my_rows], local_sem.at[4]),
        pltpu.make_async_copy(wu_ref, wu2.at[my_rows], local_sem.at[5]),
        pltpu.make_async_copy(wd_ref, wd2.at[my_rows], local_sem.at[6]),
    ]
    for one in loads:
        one.start()

    barrier = pltpu.get_barrier_semaphore()
    peers = [sibling, across, up_y, down_y, up_x, down_x] + zl_peers
    for peer in peers:
        pl.semaphore_signal(barrier, inc=1, device_id=peer, device_id_type=MESH)
    pl.semaphore_wait(barrier, len(peers))

    loads[0].wait()
    loads[1].wait()
    kv_id = numbers(17)
    ids = [kv_id(n) for n in range(17)]

    def block_at(y_, z_, k_):
        return kv.at[4 * y_ + 2 * z_ + k_]

    def half_at(y_, z_, k_, h):
        return kv.at[4 * y_ + 2 * z_ + k_, h * (KROWS // 2) : (h + 1) * (KROWS // 2)]

    own = block_at(y, z, k)
    send(own, own, across, ids[0])
    send(own, own, up_y, ids[1])
    send(own, own, down_y, ids[2])
    send(own, own, sibling, ids[3])

    for h in range(NH):
        q3[h] = q_ref[:, h * DH : (h + 1) * DH]
    m_s[...] = jnp.full(m_s.shape, BLOCKED, F32)
    l_s[...] = jnp.zeros(l_s.shape, F32)
    acc_s[...] = jnp.zeros(acc_s.shape, F32)

    def as_column(row):
        return jnp.broadcast_to(row.astype(F32), (ROWS, ROWS)).T.astype(jnp.int32)

    q_span = as_column(qspan_ref[pl.ds(c, 1), :])
    q_pos = as_column(qpos_ref[pl.ds(c, 1), :])

    def attend(group):
        visible = []
        for n in range(8):
            tile = 8 * group + n
            allowed = table_ref[c, tile] == 1
            spans = jnp.where(allowed, kspan_ref[pl.ds(tile, 1), :], -1)
            places = kpos_ref[pl.ds(tile, 1), :]
            index = tile * TILE + lax.broadcasted_iota(jnp.int32, (1, TILE), 1)
            spans = jnp.broadcast_to(spans, (ROWS, TILE))
            places = jnp.broadcast_to(places, (ROWS, TILE))
            index = jnp.broadcast_to(index, (ROWS, TILE))
            visible.append(
                jnp.where(
                    ((spans == q_span) & (places < q_pos)) | (index < SINK), 0.0, BLOCKED
                ).astype(F32)
            )
        keys = kv[pl.ds(4 * group, 4)].reshape(4 * KROWS, 2 * DH)

        def one_head(h, carry):
            scores = lax.dot_general(
                q3[h], keys[:, :DH], (((1,), (1,)), ((), ())), preferred_element_type=F32
            )
            pieces = [
                jnp.where(
                    visible[n] == 0.0,
                    scores[:, n * TILE : (n + 1) * TILE] * SCORE_SCALE,
                    BLOCKED,
                )
                for n in range(8)
            ]
            best = pieces[0]
            for piece in pieces[1:]:
                best = jnp.maximum(best, piece)
            old = m_s[h]
            new = jnp.maximum(old, jnp.max(best, axis=1, keepdims=True))
            factor = jnp.exp2(old - new)
            weights = [jnp.exp2(piece - new) for piece in pieces]
            total = weights[0]
            for one in weights[1:]:
                total = total + one
            m_s[h] = new
            l_s[h] = l_s[h] * factor + total
            rounded = jnp.concatenate([one.astype(BF16) for one in weights], axis=1)
            acc_s[h] = acc_s[h] * factor + jnp.dot(
                rounded, keys[:, DH:], preferred_element_type=F32
            )
            return carry

        lax.fori_loop(0, NH, one_head, 0)

    for one in loads[2:]:
        one.wait()
    gain = jnp.broadcast_to(gain_ref[0:1, :], (DH, COLS)).T[:, 0:1]
    for weights in (wg2, wu2):
        weights[my_rows] = (weights[my_rows].astype(F32) * gain).astype(BF16)

    other = block_at(y, zo, k)
    arrived(other, ids[0])
    send(other, other, up_y, ids[4])
    send(other, other, down_y, ids[5])
    send(other, other, sibling, ids[6])
    b = block_at(ym, z, k)
    arrived(b, ids[1])
    send(half_at(ym, z, k, 0), half_at(ym, z, k, 0), up_y, ids[7])
    send(b, b, sibling, ids[9])
    b = block_at(yp, z, k)
    arrived(b, ids[2])
    send(half_at(yp, z, k, 1), half_at(yp, z, k, 1), down_y, ids[8])
    send(b, b, sibling, ids[10])
    arrived(block_at(y, z, ko), ids[3])
    arrived(block_at(y, zo, ko), ids[6])
    attend(y)


    b = block_at(ym, zo, k)
    arrived(b, ids[4])
    send(half_at(ym, zo, k, 0), half_at(ym, zo, k, 0), up_y, ids[11])
    send(b, b, sibling, ids[13])
    b = block_at(yp, zo, k)
    arrived(b, ids[5])
    send(half_at(yp, zo, k, 1), half_at(yp, zo, k, 1), down_y, ids[12])
    send(b, b, sibling, ids[14])

    weight_id = numbers(5)
    half_rows = pl.ds(pl.multiple_of(k * COLS, COLS), COLS)
    other_rows = pl.ds(pl.multiple_of(ko * COLS, COLS), COLS)
    joint = (wo2, res2, wg2, wu2, wd2)

    arrived(block_at(ym, z, ko), ids[9])
    arrived(block_at(ym, zo, ko), ids[13])
    attend(ym)
    arrived(half_at(yo, z, k, 0), ids[7])
    arrived(half_at(yo, z, k, 1), ids[8])
    b = block_at(yo, z, k)
    send(b, b, sibling, ids[15])
    arrived(half_at(yo, zo, k, 0), ids[11])
    arrived(half_at(yo, zo, k, 1), ids[12])
    b = block_at(yo, zo, k)
    send(b, b, sibling, ids[16])
    for n, weights in enumerate(joint):
        send(weights.at[half_rows], weights.at[half_rows], sibling, weight_id(n))

    arrived(block_at(yp, z, ko), ids[10])
    arrived(block_at(yp, zo, ko), ids[14])
    attend(yp)
    arrived(block_at(yo, z, ko), ids[15])
    arrived(block_at(yo, zo, ko), ids[16])
    attend(yo)

    mine = 2 * y + z
    for h in range(NH):
        total = jnp.sum(l_s[h], axis=1, keepdims=True)
        rows = (acc_s[h] / total).astype(BF16)
        for half in range(2):
            att[half, mine, :, h * DH : (h + 1) * DH] = rows[half * HALF : (half + 1) * HALF]

    def gather_context(whole, piece, id_at, ready):
        own = whole(y, z)
        send(own, own, across, id_at(0))
        send(own, own, up_y, id_at(1))
        send(own, own, down_y, id_at(2))
        ready(y, z)
        yield
        b = whole(y, zo)
        arrived(b, id_at(0))
        send(b, b, up_y, id_at(3))
        send(b, b, down_y, id_at(4))
        for zz, first, then in ((z, 1, 5), (zo, 3, 7)):
            arrived(whole(ym, zz), id_at(first))
            send(piece(ym, zz, 0), piece(ym, zz, 0), up_y, id_at(then))
            arrived(whole(yp, zz), id_at(first + 1))
            send(piece(yp, zz, 1), piece(yp, zz, 1), down_y, id_at(then + 1))
            if first == 1:
                ready(y, zo)
            ready(ym, zz)
            ready(yp, zz)
        for zz, then in ((z, 5), (zo, 7)):
            arrived(piece(yo, zz, 0), id_at(then))
            arrived(piece(yo, zz, 1), id_at(then + 1))
            ready(yo, zz)

    def lagged(lag, work):
        waiting = []

        def add(*one):
            waiting.append(one)
            if len(waiting) > lag:
                work(*waiting.pop(0))

        def flush():
            while waiting:
                work(*waiting.pop(0))

        return add, flush

    home_j = x // 2
    plus_j, minus_j = xp // 2, xm // 2
    class Scatter:
        def __init__(self, shares, halves, fulls, out, inn, total):
            self.shares, self.halves, self.fulls = shares, halves, fulls
            self.out, self.inn, self.total = out, inn, total
            self.half_id = numbers(2, 4, 2)
            self.full_id = numbers(2, 4, 2)
            self.z_id = numbers(2, 4)

        def half(self, h, to, way):
            rows = slice(way * QUARTER, (way + 1) * QUARTER)
            return copy(
                self.shares.at[h, 2 * to + 1 - home_j, rows],
                self.halves.at[h, way, to],
                (up_x, down_x)[way],
                self.half_id(h, to, way),
            )

        def full(self, h, to, way):
            return copy(
                self.shares.at[h, 2 * to + (plus_j, minus_j)[way]],
                self.fulls.at[h, way, to],
                (up_x, down_x)[way],
                self.full_id(h, to, way),
            )

        def along_z(self, h, d):
            to = dev(zl_=lax.rem(zl + d, 4))
            return copy(self.out.at[h, d], self.inn.at[h, d], to, self.z_id(h, d))

        def ready(self, h, to, j):
            @pl.when(is_home & (j == 1 - home_j))
            def _():
                self.half(h, to, 0).start()
                self.half(h, to, 1).start()

        def relay(self, h, to, j):
            for way, at in ((0, plus_j), (1, minus_j)):
                rows = slice(way * QUARTER, (way + 1) * QUARTER)

                @pl.when(is_relay & (j == at))
                def _():
                    i = 2 * to + at
                    arrived(self.halves.at[h, way, to], self.half_id(h, to, way))
                    self.shares[h, i, rows] = (
                        self.shares[h, i, rows].astype(F32) + self.halves[h, way, to].astype(F32)
                    ).astype(BF16)
                    self.full(h, to, way).start()

        def finish_x(self, h):
            for to in (y, ym, yp, yo):
                arrived(self.fulls.at[h, 0, to], self.full_id(h, to, 0))
                arrived(self.fulls.at[h, 1, to], self.full_id(h, to, 1))
                here = (
                    self.shares[h, 2 * to + home_j].astype(F32)
                    + self.fulls[h, 0, to].astype(F32)
                    + self.fulls[h, 1, to].astype(F32)
                )

                @pl.when(to == zl)
                def _():
                    self.total[h] = here

                @pl.when(to != zl)
                def _():
                    d = lax.rem(to - zl + 4, 4)
                    self.out[h, d] = here.astype(BF16)
                    self.along_z(h, d).start()

        def finish_z(self, h):
            total = self.total[h]
            for d in (1, 3, 2):
                arrived(self.inn.at[h, d], self.z_id(h, d))
                total = total + self.inn[h, d].astype(F32)
            return total

        def wait_sends(self):
            @pl.when(is_home)
            def _():
                for h in range(2):
                    for d in range(4):
                        self.half(h, d, 0).wait_send()
                        self.half(h, d, 1).wait_send()
                    for d in (1, 2, 3):
                        self.along_z(h, d).wait_send()

            @pl.when(is_relay)
            def _():
                for h in range(2):
                    for d in range(4):
                        self.full(h, d, 0).wait_send()
                        self.full(h, d, 1).wait_send()

    projected = Scatter(part, half_in, full_in, z_out, z_in, total_s)
    arrived(wo2.at[other_rows], weight_id(0))
    def spread_attention(h):
        relay, flush = lagged(2, lambda to, j: projected.relay(h, to, j))

        def project(to, j):
            i = 2 * to + j
            part[h, i] = lax.dot_general(
                att[h, i], wo2[...], (((1,), (1,)), ((), ())), preferred_element_type=F32
            ).astype(BF16)
            projected.ready(h, to, j)
            relay(to, j)

        yield from gather_context(
            lambda y_, z_: att.at[h, 2 * y_ + z_],
            lambda y_, z_, q: att.at[h, 2 * y_ + z_, q * QUARTER : (q + 1) * QUARTER],
            numbers(9),
            project,
        )
        flush()

    rows_a, rows_b = spread_attention(0), spread_attention(1)
    next(rows_a)
    next(rows_b)
    for _ in rows_a:
        pass
    for _ in rows_b:
        pass
    arrived(wd2.at[other_rows], weight_id(4))
    wd_t[...] = wd2[...].T
    for h in range(2):
        att_out[h * HALF : (h + 1) * HALF] = att[h, mine]

    gather_z_id = numbers(2, 3)
    gather_x_id = numbers(2, 4, 2)
    gather_half_id = numbers(2, 4, 2)
    arrived(res2.at[other_rows], weight_id(1))

    def gather_z(h, d):
        own = normed.at[h, 2 * zl + home_j]
        return copy(own, own, zl_peers[d - 1], gather_z_id(h, d - 1))

    def gather_x(h, zq, way):
        b = normed.at[h, 2 * zq + home_j]
        return copy(b, b, (up_x, down_x)[way], gather_x_id(h, zq, way))

    def gather_half(h, zq, way):
        j = (minus_j, plus_j)[way]
        b = normed.at[h, 2 * zq + j, way * QUARTER : (way + 1) * QUARTER]
        return copy(b, b, (up_x, down_x)[way], gather_half_id(h, zq, way))

    def make_stream(h):
        total = projected.finish_z(h)
        normed[h, 2 * zl + home_j] = (res_s[h] + total).astype(BF16)
        for way in range(2):
            gather_x(h, zl, way).start()
        for d in (2, 1, 3):
            gather_z(h, d).start()

    @pl.when(is_home)
    def _():
        rows = res2[...].astype(F32).T
        res_s[0] = rows[:HALF]
        res_s[1] = rows[HALF:]
        projected.finish_x(0)
        make_stream(0)
        projected.finish_x(1)

    arrived(wg2.at[other_rows], weight_id(2))
    arrived(wu2.at[other_rows], weight_id(3))
    half_id = numbers(2, 2, 2)
    full_id = numbers(2, 2, 2)
    cross_id = numbers(2)
    first_j = jnp.where(is_home, home_j, minus_j)

    def y_half(h, zz, way):
        rows = slice(way * QUARTER, (way + 1) * QUARTER)
        return copy(
            gu.at[h, 2 * yo + zz, rows],
            gu_half.at[h, way, zz],
            (up_y, down_y)[way],
            half_id(h, zz, way),
        )

    def y_full(h, zz, way):
        return copy(
            gu.at[h, 2 * (yp, ym)[way] + zz],
            gu_full.at[h, way, zz],
            (up_y, down_y)[way],
            full_id(h, zz, way),
        )

    def y_cross(h):
        return copy(gu.at[h, 2 * y + zo], gu_z.at[h], across, cross_id(h))

    def gate_up(h, zq, j):
        i = 2 * zq + j
        rows = normed[h, i]
        wide = rows.astype(F32)
        squares = jnp.sum(wide * wide, axis=1, keepdims=True)
        squares = jnp.broadcast_to(squares, (HALF, WIDE - 2 * FF))
        gate = jnp.dot(rows, wg2[...], preferred_element_type=F32)
        up = jnp.dot(rows, wu2[...], preferred_element_type=F32)
        gu[h, i] = jnp.concatenate([gate, up, squares], axis=1).astype(BF16)

        @pl.when(lax.rem(zq - y + 4, 4) == 2)
        def _():
            y_half(h, j, 0).start()
            y_half(h, j, 1).start()

    def steps_back(n):
        d = jnp.where(n < 2, n, 5 - n)
        return d, lax.rem(zl + 4 - d, 4)

    def take_first(h, n):
        d, zq = steps_back(n)

        @pl.when(is_home & (n > 0))
        def _():
            arrived(normed.at[h, 2 * zq + home_j], gather_z_id(h, d - 1))
            gather_x(h, zq, 0).start()
            gather_x(h, zq, 1).start()

        @pl.when(is_relay)
        def _():
            arrived(normed.at[h, 2 * zq + minus_j], gather_x_id(h, zq, 0))
            gather_half(h, zq, 0).start()
            arrived(normed.at[h, 2 * zq + plus_j], gather_x_id(h, zq, 1))
            gather_half(h, zq, 1).start()

        gate_up(h, zq, first_j)

    def take_second(h, n):
        d, zq = steps_back(n)

        @pl.when(is_home)
        def _():
            for way in range(2):
                b = normed.at[h, 2 * zq + 1 - home_j, way * QUARTER : (way + 1) * QUARTER]
                arrived(b, gather_half_id(h, zq, way))

        gate_up(h, zq, 1 - first_j)

    def y_relay(h, n):
        d, zq = steps_back(n)
        for way, there in ((0, yp), (1, ym)):
            rows = slice(way * QUARTER, (way + 1) * QUARTER)

            @pl.when(zq == there)
            def _():
                for zz in (zo, z):
                    i = 2 * there + zz
                    arrived(gu_half.at[h, way, zz], half_id(h, zz, way))
                    gu[h, i, rows] = (
                        gu[h, i, rows].astype(F32) + gu_half[h, way, zz].astype(F32)
                    ).astype(BF16)
                    y_full(h, zz, way).start()

    def own_sum(h, zz):
        return (
            gu[h, 2 * y + zz].astype(F32)
            + gu_full[h, 0, zz].astype(F32)
            + gu_full[h, 1, zz].astype(F32)
        )

    def finish_y_across(h):
        arrived(gu_full.at[h, 0, zo], full_id(h, zo, 0))
        arrived(gu_full.at[h, 1, zo], full_id(h, zo, 1))
        gu[h, 2 * y + zo] = own_sum(h, zo).astype(BF16)
        y_cross(h).start()

    def finish_y(h):
        arrived(gu_full.at[h, 0, z], full_id(h, z, 0))
        arrived(gu_full.at[h, 1, z], full_id(h, z, 1))
        arrived(gu_z.at[h], cross_id(h))
        total = own_sum(h, z) + gu_z[h].astype(F32)
        scale = lax.rsqrt(total[:, 2 * FF : 2 * FF + 1] / D + 1e-05)
        gate, up = total[:, :FF] * scale, total[:, FF : 2 * FF] * scale
        hid[h, mine] = (gate / (1.0 + jnp.exp(-gate)) * up).astype(BF16)

    def steps_a(n, carry):
        @pl.when(n < 4)
        def _():
            take_first(0, n)

        @pl.when(is_home & (n == 3))
        def _():
            make_stream(1)

        @pl.when(n >= 1)
        def _():
            take_second(0, n - 1)

        @pl.when(n >= 3)
        def _():
            y_relay(0, n - 3)

        return carry

    def steps_b(n, carry):
        @pl.when(n < 4)
        def _():
            take_first(1, n)

        @pl.when(n < 2)
        def _():
            y_relay(0, n + 2)

        @pl.when(n >= 1)
        def _():
            take_second(1, n - 1)

        return carry

    lax.fori_loop(0, 5, steps_a, 0)
    lax.fori_loop(0, 5, steps_b, 0)
    finish_y_across(0)
    for n in range(4):
        y_relay(1, n)

    summed = Scatter(part2, half_in2, full_in2, z_out2, z_in2, total_s2)

    def spread_hidden(h):
        relay, flush = lagged(2, lambda to, j: summed.relay(h, to, j))

        def down(to, j):
            i = 2 * to + j
            part2[h, i] = jnp.dot(hid[h, i], wd_t[...], preferred_element_type=F32).astype(BF16)
            summed.ready(h, to, j)
            relay(to, j)

        yield from gather_context(
            lambda y_, z_: hid.at[h, 2 * y_ + z_],
            lambda y_, z_, q: hid.at[h, 2 * y_ + z_, q * QUARTER : (q + 1) * QUARTER],
            numbers(9),
            down,
        )
        flush()

    finish_y(0)
    spread_a, spread_b = spread_hidden(0), spread_hidden(1)
    next(spread_a)
    finish_y_across(1)
    for _ in spread_a:
        pass
    finish_y(1)
    earlier = list(sent)
    sent.clear()
    next(spread_b)
    for one in earlier:
        one.wait_send()
    projected.wait_sends()
    for h in range(2):
        for zz in range(2):
            for way in range(2):
                y_half(h, zz, way).wait_send()
                y_full(h, zz, way).wait_send()
        y_cross(h).wait_send()

    @pl.when(is_home)
    def _():
        for h in range(2):
            for d in (1, 2, 3):
                gather_z(h, d).wait_send()
            for zq in range(4):
                for way in range(2):
                    gather_x(h, zq, way).wait_send()

    @pl.when(is_relay)
    def _():
        for h in range(2):
            for zq in range(4):
                for way in range(2):
                    gather_half(h, zq, way).wait_send()


    for _ in spread_b:
        pass

    mix_id = numbers(1)(0)
    mix_mine = mix_t.at[other_rows]

    @pl.when(is_home)
    def _():
        summed.finish_x(0)
        summed.finish_x(1)
        mixed_s[0] = normed[0, 2 * zl + home_j].astype(F32) + summed.finish_z(0)
        mixed_s[1] = normed[1, 2 * zl + home_j].astype(F32) + summed.finish_z(1)
        mixed = jnp.concatenate([mixed_s[0], mixed_s[1]], axis=0)
        mix_t[...] = mixed.T.astype(BF16)
        copy(mix_mine, mix_recv, sibling, mix_id).start()
        mix_out[...] = mix_t[half_rows]
        copy(mix_mine, mix_recv, sibling, mix_id).wait_send()

    @pl.when(is_relay)
    def _():
        arrived(mix_recv, mix_id)
        mix_out[...] = mix_recv[...]

    for one in sent:
        one.wait_send()
    summed.wait_sends()
    assert count[0] <= N_COPIES


def local(
    queries,
    context_keys,
    context_values,
    query_span,
    query_position,
    key_span,
    key_position,
    tile_table,
    residual,
    out_weight,
    norm_gain,
    gate_weight,
    up_weight,
    down_weight,
):
    vmem = pl.BlockSpec(memory_space=pltpu.VMEM)
    smem = pl.BlockSpec(memory_space=pltpu.SMEM)
    hbm = pl.BlockSpec(memory_space=pl.ANY)
    gain = jnp.broadcast_to(norm_gain.astype(F32)[None, :], (8, COLS))
    def stages():
        return [
            pltpu.VMEM((2, BLOCKS, HALF, CC), BF16),
            pltpu.VMEM((2, 2, 4, QUARTER, CC), BF16),
            pltpu.VMEM((2, 2, 4, HALF, CC), BF16),
            pltpu.VMEM((2, 4, HALF, CC), BF16),
            pltpu.VMEM((2, 4, HALF, CC), BF16),
            pltpu.VMEM((2, HALF, CC), F32),
        ]

    scratch = [
        pltpu.VMEM((16, KROWS, 2 * DH), BF16),
        pltpu.VMEM((NH, ROWS, DH), BF16),
        pltpu.VMEM((NH, ROWS, DH), F32),
        pltpu.VMEM((NH, ROWS, DH), F32),
        pltpu.VMEM((NH, ROWS, DH), F32),
        pltpu.VMEM((2, BLOCKS, HALF, NH * DH), BF16),
        pltpu.VMEM((CC, NH * DH), BF16),
        pltpu.VMEM((CC, FF), BF16),
        pltpu.VMEM((CC, FF), BF16),
        pltpu.VMEM((CC, FF), BF16),
        pltpu.VMEM((CC, ROWS), BF16),
        pltpu.VMEM((2, HALF, CC), F32),
        *stages(),
        pltpu.VMEM((2, BLOCKS, HALF, CC), BF16),
        pltpu.VMEM((2, BLOCKS, HALF, WIDE), BF16),
        pltpu.VMEM((2, 2, 2, QUARTER, WIDE), BF16),
        pltpu.VMEM((2, 2, 2, HALF, WIDE), BF16),
        pltpu.VMEM((2, HALF, WIDE), BF16),
        pltpu.VMEM((2, BLOCKS, HALF, FF), BF16),
        *stages(),
        pltpu.VMEM((FF, CC), BF16),
        pltpu.VMEM((2, HALF, CC), F32),
        pltpu.VMEM((CC, ROWS), BF16),
        pltpu.VMEM((COLS, ROWS), BF16),
        pltpu.SemaphoreType.DMA((N_COPIES,)),
        pltpu.SemaphoreType.DMA((N_COPIES,)),
        pltpu.SemaphoreType.DMA((8,)),
    ]
    attention, mixed = pl.pallas_call(
        layer_kernel,
        out_shape=(
            jax.ShapeDtypeStruct(queries.shape, BF16),
            jax.ShapeDtypeStruct(residual.shape[::-1], BF16),
        ),
        in_specs=[vmem, hbm, hbm, vmem, vmem, vmem, vmem, smem, hbm, hbm, vmem, hbm, hbm, hbm],
        out_specs=(vmem, vmem),
        scratch_shapes=scratch,
        compiler_params=pltpu.CompilerParams(
            collective_id=0, has_side_effects=True, vmem_limit_bytes=60 * 2**20
        ),
        cost_estimate=pl.CostEstimate(
            flops=9_000_000_000, bytes_accessed=8_000_000, transcendentals=2_000_000
        ),
        name="layer",
    )(
        queries,
        context_keys,
        context_values,
        query_span.reshape(16, TILE),
        query_position.reshape(16, TILE),
        key_span.reshape(32, TILE),
        key_position.reshape(32, TILE),
        tile_table,
        residual.T,
        out_weight.T,
        gain,
        gate_weight,
        up_weight,
        down_weight.T,
    )
    return attention, mixed.T


def solution(mesh):
    placed = (
        P("context", "tensor"),
        P("context", None),
        P("context", None),
        P(),
        P(),
        P(),
        P(),
        P(),
        P("tensor", "context"),
        P("tensor", "context"),
        P("context"),
        P("context", "tensor"),
        P("context", "tensor"),
        P("tensor", "context"),
    )
    return jax.shard_map(
        local,
        mesh=mesh,
        in_specs=placed,
        out_specs=(P("context", "tensor"), P("tensor", "context")),
        check_vma=False,
    )
```

```python
import math

import jax
import jax.numpy as jnp
from jax import lax
from jax.experimental import pallas as pl
from jax.experimental.pallas import tpu as pltpu
from jax.sharding import PartitionSpec as P

MESH = pl.DeviceIdType.MESH
F32 = jnp.float32
BF16 = jnp.bfloat16

D = 7168
DH = 128
TILE = 128
SINK = 4
ROWS = 128
HALF = ROWS // 2
QUARTER = HALF // 2
NH = 3
KROWS = 256
COLS = 448
CC = 2 * COLS
FF = 1200
WIDE = 2432
BLOCKS = 8

BLOCKED = -1e30
SCORE_SCALE = math.log2(math.e) / math.sqrt(DH)

N_COPIES = 260


def layer_kernel(
    q_ref,
    key_ref,
    value_ref,
    qspan_ref,
    qpos_ref,
    kspan_ref,
    kpos_ref,
    table_ref,
    res_ref,
    wo_ref,
    gain_ref,
    wg_ref,
    wu_ref,
    wd_ref,
    att_out,
    mix_out,
    kv,
    q3,
    m_s,
    l_s,
    acc_s,
    att,
    wo2,
    wd2,
    wg2,
    wu2,
    res2,
    res_s,
    part,
    half_in,
    full_in,
    z_out,
    z_in,
    total_s,
    normed,
    gu,
    gu_half,
    gu_full,
    gu_z,
    hid,
    part2,
    half_in2,
    full_in2,
    z_out2,
    z_in2,
    total_s2,
    wd_t,
    mixed_s,
    mix_t,
    mix_recv,
    send_sem,
    recv_sem,
    local_sem,
):
    c = lax.axis_index("context")
    t = lax.axis_index("tensor")
    y, z, k = c // 4, lax.rem(c // 2, 2), lax.rem(c, 2)
    zl, x = t // 4, lax.rem(t, 4)
    yp, ym, yo = lax.rem(y + 1, 4), lax.rem(y + 3, 4), lax.rem(y + 2, 4)
    xp, xm = lax.rem(x + 1, 4), lax.rem(x + 3, 4)
    zo, ko = 1 - z, 1 - k

    def dev(y_=None, z_=None, k_=None, zl_=None, x_=None):
        y_ = y if y_ is None else y_
        z_ = z if z_ is None else z_
        k_ = k if k_ is None else k_
        zl_ = zl if zl_ is None else zl_
        x_ = x if x_ is None else x_
        return (4 * y_ + 2 * z_ + k_, 4 * zl_ + x_)

    sibling, across = dev(k_=ko), dev(z_=zo)
    up_y, down_y = dev(y_=yp), dev(y_=ym)
    up_x, down_x = dev(x_=xp), dev(x_=xm)
    zl_peers = [dev(zl_=lax.rem(zl + d, 4)) for d in (1, 2, 3)]
    is_home = lax.rem(x + k, 2) == 0
    is_relay = lax.rem(x + k, 2) == 1

    count = [0]
    sent = []

    def numbers(*shape):
        base = count[0]
        count[0] += math.prod(shape)

        def at(*index):
            flat = 0
            for size, one in zip(shape, index):
                flat = flat * size + one
            return base + flat

        return at

    def copy(src, dst, to, number):
        return pltpu.make_async_remote_copy(
            src_ref=src,
            dst_ref=dst,
            send_sem=send_sem.at[number],
            recv_sem=recv_sem.at[number],
            device_id=to,
            device_id_type=MESH,
        )

    def send(src, dst, to, number):
        one = copy(src, dst, to, number)
        one.start()
        sent.append(one)

    def arrived(dst, number):
        copy(dst, dst, sibling, number).wait_recv()

    kv_head = t // 2
    head_columns = pl.ds(pl.multiple_of(kv_head * DH, DH), DH)
    my_rows = pl.ds(pl.multiple_of(k * COLS, COLS), COLS)
    loads = [
        pltpu.make_async_copy(key_ref.at[:, head_columns], kv.at[c, :, 0:DH], local_sem.at[0]),
        pltpu.make_async_copy(
            value_ref.at[:, head_columns], kv.at[c, :, DH : 2 * DH], local_sem.at[1]
        ),
        pltpu.make_async_copy(wo_ref, wo2.at[my_rows], local_sem.at[2]),
        pltpu.make_async_copy(res_ref, res2.at[my_rows], local_sem.at[3]),
        pltpu.make_async_copy(wg_ref, wg2.at[my_rows], local_sem.at[4]),
        pltpu.make_async_copy(wu_ref, wu2.at[my_rows], local_sem.at[5]),
        pltpu.make_async_copy(wd_ref, wd2.at[my_rows], local_sem.at[6]),
    ]
    for one in loads:
        one.start()

    barrier = pltpu.get_barrier_semaphore()
    peers = [sibling, across, up_y, down_y, up_x, down_x] + zl_peers
    for peer in peers:
        pl.semaphore_signal(barrier, inc=1, device_id=peer, device_id_type=MESH)
    pl.semaphore_wait(barrier, len(peers))

    loads[0].wait()
    loads[1].wait()
    kv_id = numbers(17)
    ids = [kv_id(n) for n in range(17)]

    def block_at(y_, z_, k_):
        return kv.at[4 * y_ + 2 * z_ + k_]

    def half_at(y_, z_, k_, h):
        return kv.at[4 * y_ + 2 * z_ + k_, h * (KROWS // 2) : (h + 1) * (KROWS // 2)]

    own = block_at(y, z, k)
    send(own, own, across, ids[0])
    send(own, own, up_y, ids[1])
    send(own, own, down_y, ids[2])
    send(own, own, sibling, ids[3])

    for h in range(NH):
        q3[h] = q_ref[:, h * DH : (h + 1) * DH]
    m_s[...] = jnp.full(m_s.shape, BLOCKED, F32)
    l_s[...] = jnp.zeros(l_s.shape, F32)
    acc_s[...] = jnp.zeros(acc_s.shape, F32)

    def as_column(row):
        return jnp.broadcast_to(row.astype(F32), (ROWS, ROWS)).T.astype(jnp.int32)

    q_span = as_column(qspan_ref[pl.ds(c, 1), :])
    q_pos = as_column(qpos_ref[pl.ds(c, 1), :])

    def attend(group):
        visible = []
        for n in range(8):
            tile = 8 * group + n
            allowed = table_ref[c, tile] == 1
            spans = jnp.where(allowed, kspan_ref[pl.ds(tile, 1), :], -1)
            places = kpos_ref[pl.ds(tile, 1), :]
            index = tile * TILE + lax.broadcasted_iota(jnp.int32, (1, TILE), 1)
            spans = jnp.broadcast_to(spans, (ROWS, TILE))
            places = jnp.broadcast_to(places, (ROWS, TILE))
            index = jnp.broadcast_to(index, (ROWS, TILE))
            visible.append(
                jnp.where(
                    ((spans == q_span) & (places < q_pos)) | (index < SINK), 0.0, BLOCKED
                ).astype(F32)
            )
        keys = kv[pl.ds(4 * group, 4)].reshape(4 * KROWS, 2 * DH)

        def one_head(h, carry):
            scores = lax.dot_general(
                q3[h], keys[:, :DH], (((1,), (1,)), ((), ())), preferred_element_type=F32
            )
            pieces = [
                jnp.where(
                    visible[n] == 0.0,
                    scores[:, n * TILE : (n + 1) * TILE] * SCORE_SCALE,
                    BLOCKED,
                )
                for n in range(8)
            ]
            best = pieces[0]
            for piece in pieces[1:]:
                best = jnp.maximum(best, piece)
            old = m_s[h]
            new = jnp.maximum(old, jnp.max(best, axis=1, keepdims=True))
            factor = jnp.exp2(old - new)
            weights = [jnp.exp2(piece - new) for piece in pieces]
            total = weights[0]
            for one in weights[1:]:
                total = total + one
            m_s[h] = new
            l_s[h] = l_s[h] * factor + total
            rounded = jnp.concatenate([one.astype(BF16) for one in weights], axis=1)
            acc_s[h] = acc_s[h] * factor + jnp.dot(
                rounded, keys[:, DH:], preferred_element_type=F32
            )
            return carry

        lax.fori_loop(0, NH, one_head, 0)

    for one in loads[2:]:
        one.wait()
    gain = jnp.broadcast_to(gain_ref[0:1, :], (DH, COLS)).T[:, 0:1]
    for weights in (wg2, wu2):
        weights[my_rows] = (weights[my_rows].astype(F32) * gain).astype(BF16)

    other = block_at(y, zo, k)
    arrived(other, ids[0])
    send(other, other, up_y, ids[4])
    send(other, other, down_y, ids[5])
    send(other, other, sibling, ids[6])
    b = block_at(ym, z, k)
    arrived(b, ids[1])
    send(half_at(ym, z, k, 0), half_at(ym, z, k, 0), up_y, ids[7])
    send(b, b, sibling, ids[9])
    b = block_at(yp, z, k)
    arrived(b, ids[2])
    send(half_at(yp, z, k, 1), half_at(yp, z, k, 1), down_y, ids[8])
    send(b, b, sibling, ids[10])
    arrived(block_at(y, z, ko), ids[3])
    arrived(block_at(y, zo, ko), ids[6])
    attend(y)


    b = block_at(ym, zo, k)
    arrived(b, ids[4])
    send(half_at(ym, zo, k, 0), half_at(ym, zo, k, 0), up_y, ids[11])
    send(b, b, sibling, ids[13])
    b = block_at(yp, zo, k)
    arrived(b, ids[5])
    send(half_at(yp, zo, k, 1), half_at(yp, zo, k, 1), down_y, ids[12])
    send(b, b, sibling, ids[14])

    weight_id = numbers(5)
    half_rows = pl.ds(pl.multiple_of(k * COLS, COLS), COLS)
    other_rows = pl.ds(pl.multiple_of(ko * COLS, COLS), COLS)
    joint = (wo2, res2, wg2, wu2, wd2)

    arrived(block_at(ym, z, ko), ids[9])
    arrived(block_at(ym, zo, ko), ids[13])
    attend(ym)
    arrived(half_at(yo, z, k, 0), ids[7])
    arrived(half_at(yo, z, k, 1), ids[8])
    b = block_at(yo, z, k)
    send(b, b, sibling, ids[15])
    arrived(half_at(yo, zo, k, 0), ids[11])
    arrived(half_at(yo, zo, k, 1), ids[12])
    b = block_at(yo, zo, k)
    send(b, b, sibling, ids[16])
    for n, weights in enumerate(joint):
        send(weights.at[half_rows], weights.at[half_rows], sibling, weight_id(n))

    arrived(block_at(yp, z, ko), ids[10])
    arrived(block_at(yp, zo, ko), ids[14])
    attend(yp)
    arrived(block_at(yo, z, ko), ids[15])
    arrived(block_at(yo, zo, ko), ids[16])
    attend(yo)

    mine = 2 * y + z
    for h in range(NH):
        total = jnp.sum(l_s[h], axis=1, keepdims=True)
        rows = (acc_s[h] / total).astype(BF16)
        for half in range(2):
            att[half, mine, :, h * DH : (h + 1) * DH] = rows[half * HALF : (half + 1) * HALF]

    def gather_context(whole, piece, id_at, ready):
        own = whole(y, z)
        send(own, own, across, id_at(0))
        send(own, own, up_y, id_at(1))
        send(own, own, down_y, id_at(2))
        ready(y, z)
        yield
        b = whole(y, zo)
        arrived(b, id_at(0))
        send(b, b, up_y, id_at(3))
        send(b, b, down_y, id_at(4))
        for zz, first, then in ((z, 1, 5), (zo, 3, 7)):
            arrived(whole(ym, zz), id_at(first))
            send(piece(ym, zz, 0), piece(ym, zz, 0), up_y, id_at(then))
            arrived(whole(yp, zz), id_at(first + 1))
            send(piece(yp, zz, 1), piece(yp, zz, 1), down_y, id_at(then + 1))
            if first == 1:
                ready(y, zo)
            ready(ym, zz)
            ready(yp, zz)
        for zz, then in ((z, 5), (zo, 7)):
            arrived(piece(yo, zz, 0), id_at(then))
            arrived(piece(yo, zz, 1), id_at(then + 1))
            ready(yo, zz)

    def lagged(lag, work):
        waiting = []

        def add(*one):
            waiting.append(one)
            if len(waiting) > lag:
                work(*waiting.pop(0))

        def flush():
            while waiting:
                work(*waiting.pop(0))

        return add, flush

    home_j = x // 2
    plus_j, minus_j = xp // 2, xm // 2
    class Scatter:
        def __init__(self, shares, halves, fulls, out, inn, total):
            self.shares, self.halves, self.fulls = shares, halves, fulls
            self.out, self.inn, self.total = out, inn, total
            self.half_id = numbers(2, 4, 2)
            self.full_id = numbers(2, 4, 2)
            self.z_id = numbers(2, 4)

        def half(self, h, to, way):
            rows = slice(way * QUARTER, (way + 1) * QUARTER)
            return copy(
                self.shares.at[h, 2 * to + 1 - home_j, rows],
                self.halves.at[h, way, to],
                (up_x, down_x)[way],
                self.half_id(h, to, way),
            )

        def full(self, h, to, way):
            return copy(
                self.shares.at[h, 2 * to + (plus_j, minus_j)[way]],
                self.fulls.at[h, way, to],
                (up_x, down_x)[way],
                self.full_id(h, to, way),
            )

        def along_z(self, h, d):
            to = dev(zl_=lax.rem(zl + d, 4))
            return copy(self.out.at[h, d], self.inn.at[h, d], to, self.z_id(h, d))

        def ready(self, h, to, j):
            @pl.when(is_home & (j == 1 - home_j))
            def _():
                self.half(h, to, 0).start()
                self.half(h, to, 1).start()

        def relay(self, h, to, j):
            for way, at in ((0, plus_j), (1, minus_j)):
                rows = slice(way * QUARTER, (way + 1) * QUARTER)

                @pl.when(is_relay & (j == at))
                def _():
                    i = 2 * to + at
                    arrived(self.halves.at[h, way, to], self.half_id(h, to, way))
                    self.shares[h, i, rows] = (
                        self.shares[h, i, rows].astype(F32) + self.halves[h, way, to].astype(F32)
                    ).astype(BF16)
                    self.full(h, to, way).start()

        def finish_x(self, h):
            for to in (y, ym, yp, yo):
                arrived(self.fulls.at[h, 0, to], self.full_id(h, to, 0))
                arrived(self.fulls.at[h, 1, to], self.full_id(h, to, 1))
                here = (
                    self.shares[h, 2 * to + home_j].astype(F32)
                    + self.fulls[h, 0, to].astype(F32)
                    + self.fulls[h, 1, to].astype(F32)
                )

                @pl.when(to == zl)
                def _():
                    self.total[h] = here

                @pl.when(to != zl)
                def _():
                    d = lax.rem(to - zl + 4, 4)
                    self.out[h, d] = here.astype(BF16)
                    self.along_z(h, d).start()

        def finish_z(self, h):
            total = self.total[h]
            for d in (1, 3, 2):
                arrived(self.inn.at[h, d], self.z_id(h, d))
                total = total + self.inn[h, d].astype(F32)
            return total

        def wait_sends(self):
            @pl.when(is_home)
            def _():
                for h in range(2):
                    for d in range(4):
                        self.half(h, d, 0).wait_send()
                        self.half(h, d, 1).wait_send()
                    for d in (1, 2, 3):
                        self.along_z(h, d).wait_send()

            @pl.when(is_relay)
            def _():
                for h in range(2):
                    for d in range(4):
                        self.full(h, d, 0).wait_send()
                        self.full(h, d, 1).wait_send()

    projected = Scatter(part, half_in, full_in, z_out, z_in, total_s)
    arrived(wo2.at[other_rows], weight_id(0))
    def spread_attention(h):
        relay, flush = lagged(2, lambda to, j: projected.relay(h, to, j))

        def project(to, j):
            i = 2 * to + j
            part[h, i] = lax.dot_general(
                att[h, i], wo2[...], (((1,), (1,)), ((), ())), preferred_element_type=F32
            ).astype(BF16)
            projected.ready(h, to, j)
            relay(to, j)

        yield from gather_context(
            lambda y_, z_: att.at[h, 2 * y_ + z_],
            lambda y_, z_, q: att.at[h, 2 * y_ + z_, q * QUARTER : (q + 1) * QUARTER],
            numbers(9),
            project,
        )
        flush()

    rows_a, rows_b = spread_attention(0), spread_attention(1)
    next(rows_a)
    next(rows_b)
    for _ in rows_a:
        pass
    for _ in rows_b:
        pass
    arrived(wd2.at[other_rows], weight_id(4))
    wd_t[...] = wd2[...].T
    for h in range(2):
        att_out[h * HALF : (h + 1) * HALF] = att[h, mine]

    gather_z_id = numbers(2, 3)
    gather_x_id = numbers(2, 4, 2)
    gather_half_id = numbers(2, 4, 2)
    arrived(res2.at[other_rows], weight_id(1))

    def gather_z(h, d):
        own = normed.at[h, 2 * zl + home_j]
        return copy(own, own, zl_peers[d - 1], gather_z_id(h, d - 1))

    def gather_x(h, zq, way):
        b = normed.at[h, 2 * zq + home_j]
        return copy(b, b, (up_x, down_x)[way], gather_x_id(h, zq, way))

    def gather_half(h, zq, way):
        j = (minus_j, plus_j)[way]
        b = normed.at[h, 2 * zq + j, way * QUARTER : (way + 1) * QUARTER]
        return copy(b, b, (up_x, down_x)[way], gather_half_id(h, zq, way))

    def make_stream(h):
        total = projected.finish_z(h)
        normed[h, 2 * zl + home_j] = (res_s[h] + total).astype(BF16)
        for way in range(2):
            gather_x(h, zl, way).start()
        for d in (2, 1, 3):
            gather_z(h, d).start()

    @pl.when(is_home)
    def _():
        rows = res2[...].astype(F32).T
        res_s[0] = rows[:HALF]
        res_s[1] = rows[HALF:]
        projected.finish_x(0)
        make_stream(0)
        projected.finish_x(1)

    arrived(wg2.at[other_rows], weight_id(2))
    arrived(wu2.at[other_rows], weight_id(3))
    half_id = numbers(2, 2, 2)
    full_id = numbers(2, 2, 2)
    cross_id = numbers(2)
    first_j = jnp.where(is_home, home_j, minus_j)

    def y_half(h, zz, way):
        rows = slice(way * QUARTER, (way + 1) * QUARTER)
        return copy(
            gu.at[h, 2 * yo + zz, rows],
            gu_half.at[h, way, zz],
            (up_y, down_y)[way],
            half_id(h, zz, way),
        )

    def y_full(h, zz, way):
        return copy(
            gu.at[h, 2 * (yp, ym)[way] + zz],
            gu_full.at[h, way, zz],
            (up_y, down_y)[way],
            full_id(h, zz, way),
        )

    def y_cross(h):
        return copy(gu.at[h, 2 * y + zo], gu_z.at[h], across, cross_id(h))

    def gate_up(h, zq, j):
        i = 2 * zq + j
        rows = normed[h, i]
        wide = rows.astype(F32)
        squares = jnp.sum(wide * wide, axis=1, keepdims=True)
        squares = jnp.broadcast_to(squares, (HALF, WIDE - 2 * FF))
        gate = jnp.dot(rows, wg2[...], preferred_element_type=F32)
        up = jnp.dot(rows, wu2[...], preferred_element_type=F32)
        gu[h, i] = jnp.concatenate([gate, up, squares], axis=1).astype(BF16)

        @pl.when(lax.rem(zq - y + 4, 4) == 2)
        def _():
            y_half(h, j, 0).start()
            y_half(h, j, 1).start()

    def steps_back(n):
        d = jnp.where(n < 2, n, 5 - n)
        return d, lax.rem(zl + 4 - d, 4)

    def take_first(h, n):
        d, zq = steps_back(n)

        @pl.when(is_home & (n > 0))
        def _():
            arrived(normed.at[h, 2 * zq + home_j], gather_z_id(h, d - 1))
            gather_x(h, zq, 0).start()
            gather_x(h, zq, 1).start()

        @pl.when(is_relay)
        def _():
            arrived(normed.at[h, 2 * zq + minus_j], gather_x_id(h, zq, 0))
            gather_half(h, zq, 0).start()
            arrived(normed.at[h, 2 * zq + plus_j], gather_x_id(h, zq, 1))
            gather_half(h, zq, 1).start()

        gate_up(h, zq, first_j)

    def take_second(h, n):
        d, zq = steps_back(n)

        @pl.when(is_home)
        def _():
            for way in range(2):
                b = normed.at[h, 2 * zq + 1 - home_j, way * QUARTER : (way + 1) * QUARTER]
                arrived(b, gather_half_id(h, zq, way))

        gate_up(h, zq, 1 - first_j)

    def y_relay(h, n):
        d, zq = steps_back(n)
        for way, there in ((0, yp), (1, ym)):
            rows = slice(way * QUARTER, (way + 1) * QUARTER)

            @pl.when(zq == there)
            def _():
                for zz in (zo, z):
                    i = 2 * there + zz
                    arrived(gu_half.at[h, way, zz], half_id(h, zz, way))
                    gu[h, i, rows] = (
                        gu[h, i, rows].astype(F32) + gu_half[h, way, zz].astype(F32)
                    ).astype(BF16)
                    y_full(h, zz, way).start()

    def own_sum(h, zz):
        return (
            gu[h, 2 * y + zz].astype(F32)
            + gu_full[h, 0, zz].astype(F32)
            + gu_full[h, 1, zz].astype(F32)
        )

    def finish_y_across(h):
        arrived(gu_full.at[h, 0, zo], full_id(h, zo, 0))
        arrived(gu_full.at[h, 1, zo], full_id(h, zo, 1))
        gu[h, 2 * y + zo] = own_sum(h, zo).astype(BF16)
        y_cross(h).start()

    def finish_y(h):
        arrived(gu_full.at[h, 0, z], full_id(h, z, 0))
        arrived(gu_full.at[h, 1, z], full_id(h, z, 1))
        arrived(gu_z.at[h], cross_id(h))
        total = own_sum(h, z) + gu_z[h].astype(F32)
        scale = lax.rsqrt(total[:, 2 * FF : 2 * FF + 1] / D + 1e-05)
        gate, up = total[:, :FF] * scale, total[:, FF : 2 * FF] * scale
        hid[h, mine] = (gate / (1.0 + jnp.exp(-gate)) * up).astype(BF16)

    def steps_a(n, carry):
        @pl.when(n < 4)
        def _():
            take_first(0, n)

        @pl.when(is_home & (n == 3))
        def _():
            make_stream(1)

        @pl.when(n >= 1)
        def _():
            take_second(0, n - 1)

        @pl.when(n >= 3)
        def _():
            y_relay(0, n - 3)

        return carry

    def steps_b(n, carry):
        @pl.when(n < 4)
        def _():
            take_first(1, n)

        @pl.when(n < 2)
        def _():
            y_relay(0, n + 2)

        @pl.when(n == 4)
        def _():
            finish_y_across(0)

        @pl.when(n >= 1)
        def _():
            take_second(1, n - 1)

        return carry

    lax.fori_loop(0, 5, steps_a, 0)
    lax.fori_loop(0, 5, steps_b, 0)
    for n in range(4):
        y_relay(1, n)

    summed = Scatter(part2, half_in2, full_in2, z_out2, z_in2, total_s2)

    def spread_hidden(h):
        relay, flush = lagged(2, lambda to, j: summed.relay(h, to, j))

        def down(to, j):
            i = 2 * to + j
            part2[h, i] = jnp.dot(hid[h, i], wd_t[...], preferred_element_type=F32).astype(BF16)
            summed.ready(h, to, j)
            relay(to, j)

        yield from gather_context(
            lambda y_, z_: hid.at[h, 2 * y_ + z_],
            lambda y_, z_, q: hid.at[h, 2 * y_ + z_, q * QUARTER : (q + 1) * QUARTER],
            numbers(9),
            down,
        )
        flush()

    finish_y(0)
    spread_a, spread_b = spread_hidden(0), spread_hidden(1)
    next(spread_a)
    finish_y_across(1)
    for _ in spread_a:
        pass
    finish_y(1)
    earlier = list(sent)
    sent.clear()
    next(spread_b)
    for one in earlier:
        one.wait_send()
    projected.wait_sends()
    for h in range(2):
        for zz in range(2):
            for way in range(2):
                y_half(h, zz, way).wait_send()
                y_full(h, zz, way).wait_send()
        y_cross(h).wait_send()

    @pl.when(is_home)
    def _():
        for h in range(2):
            for d in (1, 2, 3):
                gather_z(h, d).wait_send()
            for zq in range(4):
                for way in range(2):
                    gather_x(h, zq, way).wait_send()

    @pl.when(is_relay)
    def _():
        for h in range(2):
            for zq in range(4):
                for way in range(2):
                    gather_half(h, zq, way).wait_send()


    for _ in spread_b:
        pass

    mix_id = numbers(1)(0)
    mix_mine = mix_t.at[other_rows]

    @pl.when(is_home)
    def _():
        summed.finish_x(0)
        summed.finish_x(1)
        mixed_s[0] = normed[0, 2 * zl + home_j].astype(F32) + summed.finish_z(0)
        mixed_s[1] = normed[1, 2 * zl + home_j].astype(F32) + summed.finish_z(1)
        mixed = jnp.concatenate([mixed_s[0], mixed_s[1]], axis=0)
        mix_t[...] = mixed.T.astype(BF16)
        copy(mix_mine, mix_recv, sibling, mix_id).start()
        mix_out[...] = mix_t[half_rows]
        copy(mix_mine, mix_recv, sibling, mix_id).wait_send()

    @pl.when(is_relay)
    def _():
        arrived(mix_recv, mix_id)
        mix_out[...] = mix_recv[...]

    for one in sent:
        one.wait_send()
    summed.wait_sends()
    assert count[0] <= N_COPIES


def local(
    queries,
    context_keys,
    context_values,
    query_span,
    query_position,
    key_span,
    key_position,
    tile_table,
    residual,
    out_weight,
    norm_gain,
    gate_weight,
    up_weight,
    down_weight,
):
    vmem = pl.BlockSpec(memory_space=pltpu.VMEM)
    smem = pl.BlockSpec(memory_space=pltpu.SMEM)
    hbm = pl.BlockSpec(memory_space=pl.ANY)
    gain = jnp.broadcast_to(norm_gain.astype(F32)[None, :], (8, COLS))
    def stages():
        return [
            pltpu.VMEM((2, BLOCKS, HALF, CC), BF16),
            pltpu.VMEM((2, 2, 4, QUARTER, CC), BF16),
            pltpu.VMEM((2, 2, 4, HALF, CC), BF16),
            pltpu.VMEM((2, 4, HALF, CC), BF16),
            pltpu.VMEM((2, 4, HALF, CC), BF16),
            pltpu.VMEM((2, HALF, CC), F32),
        ]

    scratch = [
        pltpu.VMEM((16, KROWS, 2 * DH), BF16),
        pltpu.VMEM((NH, ROWS, DH), BF16),
        pltpu.VMEM((NH, ROWS, DH), F32),
        pltpu.VMEM((NH, ROWS, DH), F32),
        pltpu.VMEM((NH, ROWS, DH), F32),
        pltpu.VMEM((2, BLOCKS, HALF, NH * DH), BF16),
        pltpu.VMEM((CC, NH * DH), BF16),
        pltpu.VMEM((CC, FF), BF16),
        pltpu.VMEM((CC, FF), BF16),
        pltpu.VMEM((CC, FF), BF16),
        pltpu.VMEM((CC, ROWS), BF16),
        pltpu.VMEM((2, HALF, CC), F32),
        *stages(),
        pltpu.VMEM((2, BLOCKS, HALF, CC), BF16),
        pltpu.VMEM((2, BLOCKS, HALF, WIDE), BF16),
        pltpu.VMEM((2, 2, 2, QUARTER, WIDE), BF16),
        pltpu.VMEM((2, 2, 2, HALF, WIDE), BF16),
        pltpu.VMEM((2, HALF, WIDE), BF16),
        pltpu.VMEM((2, BLOCKS, HALF, FF), BF16),
        *stages(),
        pltpu.VMEM((FF, CC), BF16),
        pltpu.VMEM((2, HALF, CC), F32),
        pltpu.VMEM((CC, ROWS), BF16),
        pltpu.VMEM((COLS, ROWS), BF16),
        pltpu.SemaphoreType.DMA((N_COPIES,)),
        pltpu.SemaphoreType.DMA((N_COPIES,)),
        pltpu.SemaphoreType.DMA((8,)),
    ]
    attention, mixed = pl.pallas_call(
        layer_kernel,
        out_shape=(
            jax.ShapeDtypeStruct(queries.shape, BF16),
            jax.ShapeDtypeStruct(residual.shape[::-1], BF16),
        ),
        in_specs=[vmem, hbm, hbm, vmem, vmem, vmem, vmem, smem, hbm, hbm, vmem, hbm, hbm, hbm],
        out_specs=(vmem, vmem),
        scratch_shapes=scratch,
        compiler_params=pltpu.CompilerParams(
            collective_id=0, has_side_effects=True, vmem_limit_bytes=60 * 2**20
        ),
        cost_estimate=pl.CostEstimate(
            flops=9_000_000_000, bytes_accessed=8_000_000, transcendentals=2_000_000
        ),
        name="layer",
    )(
        queries,
        context_keys,
        context_values,
        query_span.reshape(16, TILE),
        query_position.reshape(16, TILE),
        key_span.reshape(32, TILE),
        key_position.reshape(32, TILE),
        tile_table,
        residual.T,
        out_weight.T,
        gain,
        gate_weight,
        up_weight,
        down_weight.T,
    )
    return attention, mixed.T


def solution(mesh):
    placed = (
        P("context", "tensor"),
        P("context", None),
        P("context", None),
        P(),
        P(),
        P(),
        P(),
        P(),
        P("tensor", "context"),
        P("tensor", "context"),
        P("context"),
        P("context", "tensor"),
        P("context", "tensor"),
        P("tensor", "context"),
    )
    return jax.shard_map(
        local,
        mesh=mesh,
        in_specs=placed,
        out_specs=(P("context", "tensor"), P("tensor", "context")),
        check_vma=False,
    )
```
